32 devices in a mesh: groups: 2 (over y), scen: 4 (over z), tile: 4 (over x, core).
Axes of the slice: x: 2, y: 2, z: 4, core: 2. Of those that a mesh axis runs over, the one named last changes fastest.
Arguments:
- linking: bfloat16 [64, 256, 1024], P(('groups', 'scen', 'tile')), parts along dimension 0, may hold values from -0.029907227 to 0.029907227
- scaling: float32 [64, 256], P(('groups', 'scen', 'tile')), parts along dimension 0, may hold values from 0.25 to 4
- residual: float32 [64, 256], P(('groups', 'scen', 'tile')), parts along dimension 0, may hold values from -6 to 6
- blocks: int32 [64, 8], P('groups'), parts along dimension 0, may hold values from 0 to 63, as said below
- step_dx: float32 [128, 128], P(('groups', 'scen')), parts along dimension 0, may hold values from -24 to 24
- first_diag: float32 [16384], P(('groups', 'scen')), parts along dimension 0, may hold values from 0.5 to 1.5
Outputs:
- schur: float32 [16384, 8192], P(('groups', 'scen'), 'tile'), parts along dimension 0
- back_step: float32 [64, 256], P(('groups', 'scen', 'tile')), parts along dimension 0
The draws below stay inside these ranges and needn't reach their ends.
There are 2 independent parts, one for each index of `groups`. The reference program is written for one: setup_inputs(seed, part) draws one part's arguments, and reference() takes and returns one part's arrays. A program takes and returns all parts, laid end to end along the dimension named above; each array names one. Nothing has to cross between parts.
Inputs may be any that keep to these rules, and one draw needn't show every extreme that they name: Position k of every list names a block of column group g = k mod 4, a number from g * 16 to g * 16 + 15; within its group the block lies in one of 1 runs of 16 consecutive blocks, and its number modulo 16 lies from (k // 4) * (8) to that plus 16 // 2 - 1, so the blocks of a list are distinct. Among the 8 scenarios of one scen shard (aligned runs of 8 scenarios), at each position at most 8 name a block of the same run; in every shard and at every position of a group one run, the same for the whole group and all shards, is named exactly 8 times, and the other runs share the rest as evenly as possible.
All inputs are finite; a program needn't handle non-finite values.
Results may differ from the reference program's by a relative error of at most 0.0012.
The reference program's roundings to bfloat16 on the way count: a program that leaves them out, or rounds other values in their place, can miss the bound.
Values may be sent and summed in bfloat16 or wider, within the bound.
A program may use at most 64 MiB of HBM per device.

```python
import math
import jax
import jax.numpy as jnp
from jax import lax

BW = 128
ROWS = 256
LIST = 8
NBLK = 64
NCOL = 8192
NSCEN = 32
SG = 8
CB = 16
RB = 16
OPC = 1
LPC = 2
CAPO = 8


def draw_blocks(key, part):
    key = jax.random.fold_in(key, 7)
    key_favored, key_order, key_offset = jax.random.split(key, 3)
    group_count = LIST // LPC
    favored = jax.random.randint(key_favored, (group_count,), 0, OPC)
    position = jnp.arange(LIST)
    group_of = position % group_count
    favored_pos = favored[group_of]
    slot_rank = jnp.arange(SG)
    spread = max(OPC - 1, 1)
    others = (favored_pos[:, None] + 1 + (slot_rank[None, :] - CAPO) % spread) % OPC
    base_runs = jnp.where(slot_rank[None, :] < CAPO, favored_pos[:, None], others)
    shard_count = NSCEN // SG
    order_keys = jax.random.split(key_order, shard_count * LIST)
    tiled_runs = jnp.broadcast_to(base_runs, (shard_count, LIST, SG)).reshape(shard_count * LIST, SG)
    shuffled = jax.vmap(jax.random.permutation)(order_keys, tiled_runs)
    run_index = shuffled.reshape(shard_count, LIST, SG).transpose(0, 2, 1).reshape(NSCEN, LIST)
    run_part = RB // LPC
    offset = (position // group_count)[None, :] * run_part + jax.random.randint(key_offset, (NSCEN, LIST), 0, run_part)
    return (group_of[None, :] * CB + run_index * RB + offset).astype(jnp.int32)


def block_scale(stream_key, dims, pieces, low, top_value):
    gain, own = 1.0, jax.random.fold_in(stream_key, 6)
    for axis_at, parts in pieces:
        draws = jnp.exp(jax.random.uniform(jax.random.fold_in(own, axis_at), (parts,), jnp.float32, low / len(pieces), top_value / len(pieces)))
        gain = gain * jnp.repeat(draws, dims[axis_at] // parts).reshape([-1 if axis == axis_at else 1 for axis in range(len(dims))])
    return gain


def normal_values(own_key, extent, width, limit, pieces=(), dtype=jnp.bfloat16):
    drawn = jax.random.normal(own_key, extent, jnp.float32) * width
    if len(pieces) > 0:
        drawn = block_scale(own_key, extent, pieces, -0.22, 0.18) * drawn
    return jnp.clip(drawn, min=-limit, max=limit).astype(dtype)


def setup_inputs(seed: int = 0, part: int = 0) -> dict:
    arg_keys = jax.random.split(jax.random.key(seed), 7)
    part_keys = jax.random.split(jax.random.fold_in(arg_keys[6], part), 7)
    linking = normal_values(part_keys[0], (NSCEN, ROWS, LIST * BW), 0.005, 0.029907227, ((0, 16),))
    scaling = jnp.clip(jnp.exp(math.log(4.0) - 2.7725887 * jax.random.uniform(part_keys[1], (NSCEN, ROWS), jnp.float32) ** block_scale(part_keys[1], (NSCEN, ROWS), ((0, 16),), -0.2, 0.2)), 0.25, 4.0)
    residual = normal_values(part_keys[2], (NSCEN, ROWS), 1.0, 6.0, ((0, 16),), jnp.float32)
    blocks = draw_blocks(jax.random.fold_in(jax.random.fold_in(arg_keys[6], part), 71), part)
    step_dx = normal_values(part_keys[4], (NBLK, BW), 4.0, 24.0, ((0, 4),), jnp.float32)
    first_diag = jnp.clip(0.5 + 1.0 * jax.random.uniform(part_keys[5], (NCOL,), jnp.float32) ** block_scale(part_keys[5], (NCOL,), ((0, 4),), -0.2, 0.2), 0.5, 1.5)
    return {"linking": linking, "scaling": scaling, "residual": residual, "blocks": blocks, "step_dx": step_dx, "first_diag": first_diag}


def reference(linking, scaling, residual, blocks, step_dx, first_diag):
    low_step = step_dx.astype(jnp.bfloat16)

    def add_scenario(tiles_sum, inputs):
        link_one, scale_one, resid_one, list_one = inputs
        scaled = (jnp.sqrt(scale_one)[:, None] * link_one.astype(jnp.float32)).astype(jnp.bfloat16)
        gram_full = jnp.dot(scaled.T, scaled, preferred_element_type=jnp.float32)
        gram_low = lax.optimization_barrier(gram_full.astype(jnp.bfloat16)).astype(jnp.float32)
        gram_tiles = gram_low.reshape(LIST, BW, LIST, BW).transpose(0, 2, 1, 3)
        tiles_sum = tiles_sum.at[list_one[:, None], list_one[None, :]].add(gram_tiles)
        picked = low_step[list_one].reshape(LIST * BW)
        applied = jnp.dot(link_one, picked, preferred_element_type=jnp.float32)
        back_one = scale_one * (resid_one - applied)
        return (tiles_sum, back_one)
    start_sum = jnp.zeros((NBLK, NBLK, BW, BW), jnp.float32)
    tiles_sum, back_step = lax.scan(add_scenario, start_sum, (linking, scaling, residual, blocks))
    schur = tiles_sum.transpose(0, 2, 1, 3).reshape(NCOL, NCOL)
    diag_index = jnp.arange(NCOL)
    schur = schur.at[diag_index, diag_index].add(first_diag)
    return (schur, back_step)
```

```python
import functools

import jax
import jax.numpy as jnp
from jax import lax
from jax.experimental import pallas as pl
from jax.experimental.pallas import tpu as pltpu
from jax.sharding import PartitionSpec as P

BW = 128
LIST = 8
NBLK = 64


def on_device(linking, scaling, residual, blocks, step_dx, first_diag):
    tiles_ax = lax.axis_size("tile")
    scen_ax = lax.axis_size("scen")
    here_scen = lax.axis_index("scen")
    here_tile = lax.axis_index("tile")
    held_scen = linking.shape[0]
    shard_size = tiles_ax * held_scen
    width_rows = step_dx.shape[0]
    width_cols = NBLK // tiles_ax
    per_group = LIST // tiles_ax
    owners_per = scen_ax // tiles_ax
    cap_owner = min(shard_size, (3 * shard_size + 2 * owners_per - 1) // (2 * owners_per))
    slot_count = per_group * per_group * cap_owner
    target_count = width_rows * width_cols
    own_blocks = lax.dynamic_slice_in_dim(
        blocks, (here_scen * tiles_ax + here_tile) * held_scen, held_scen, 0
    )
    low_step = step_dx.astype(jnp.bfloat16)
    full_step = lax.all_gather(low_step, "scen", axis=0, tiled=True)
    picked = full_step[own_blocks].reshape(held_scen, LIST * BW)
    applied = jnp.einsum("src,sc->sr", linking, picked, preferred_element_type=jnp.float32)
    back_step = scaling * (residual - applied)
    scaled = (jnp.sqrt(scaling)[:, :, None] * linking).astype(jnp.bfloat16)
    gram_full = jnp.einsum("sra,src->sac", scaled, scaled, preferred_element_type=jnp.float32)
    gram_tiles = (
        gram_full.reshape(held_scen, LIST, BW, LIST, BW)
        .transpose(0, 1, 3, 2, 4)
        .astype(jnp.bfloat16)
    )
    outgoing = gram_tiles.reshape(held_scen, LIST, per_group, tiles_ax, BW, BW).transpose(
        3, 0, 2, 1, 4, 5
    )
    incoming = lax.all_to_all(outgoing, "tile", split_axis=0, concat_axis=0, tiled=True)
    flat_tiles = incoming.reshape(shard_size * per_group * LIST, BW, BW)
    shard_blocks = blocks.reshape(scen_ax, shard_size, LIST)

    def route_tiles(block_lists):
        col_blocks = jnp.take(block_lists, jnp.arange(per_group) * tiles_ax + here_tile, axis=1)
        row_block = jnp.broadcast_to(
            block_lists[:, None, :], (shard_size, per_group, LIST)
        ).reshape(-1)
        col_block = jnp.broadcast_to(col_blocks[:, :, None], (shard_size, per_group, LIST)).reshape(
            -1
        )
        owner_idx = row_block // width_rows
        hit_table = (owner_idx[:, None] == jnp.arange(scen_ax)[None, :]).astype(jnp.int32)
        before = jnp.cumsum(hit_table, axis=0) - hit_table
        slot_rank = jnp.sum(before * hit_table, axis=1)
        target = row_block % width_rows * width_cols + col_block % width_cols
        return (owner_idx, slot_rank, target)

    own_lists = lax.dynamic_index_in_dim(shard_blocks, here_scen, 0, keepdims=False)
    send_owner, send_rank, unused = route_tiles(own_lists)
    outbox = (
        jnp.zeros((scen_ax, slot_count, BW, BW), jnp.bfloat16)
        .at[send_owner, send_rank]
        .set(flat_tiles)
    )
    received = lax.all_to_all(outbox, "scen", split_axis=0, concat_axis=0, tiled=True)
    all_owner, all_rank, all_target = jax.vmap(route_tiles)(shard_blocks)
    is_mine = all_owner == here_scen
    slot_id = jnp.arange(scen_ax)[:, None] * slot_count + all_rank
    pick_target = (
        (all_target[:, :, None] == jnp.arange(target_count)[None, None, :]) & is_mine[:, :, None]
    ).astype(jnp.float32)
    pick_slot = (slot_id[:, :, None] == jnp.arange(scen_ax * slot_count)[None, None, :]).astype(
        jnp.float32
    )
    select = jnp.einsum("pnt,pnz->tz", pick_target, pick_slot).astype(jnp.bfloat16)
    summed = jnp.dot(
        select, received.reshape(scen_ax * slot_count, BW * BW), preferred_element_type=jnp.float32
    )
    schur_block = (
        summed.reshape(width_rows, width_cols, BW, BW)
        .transpose(0, 2, 1, 3)
        .reshape(width_rows * BW, width_cols * BW)
    )
    rows_global = here_scen * (width_rows * BW) + jnp.arange(width_rows * BW)
    cols_global = here_tile * (width_cols * BW) + jnp.arange(width_cols * BW)
    schur_block = schur_block + jnp.where(
        rows_global[:, None] == cols_global[None, :], first_diag[:, None], 0.0
    )
    return (schur_block, back_step)


MESH = pl.DeviceIdType.MESH


def exchange_kernel(
    n, held, scaled_ref, step_ref, got_ref, steps_ref,
    gathered, parts, step_box,
    load_sem, own_sem, pass_sem, chain_sem, part_sem, got_sem, keep_sem, step_sem, step_got_sem,
):
    z = lax.axis_index("scen")
    t = lax.axis_index("tile")

    def load(j):
        return pltpu.make_async_copy(scaled_ref.at[j], gathered.at[z, j], load_sem.at[j])

    def hop(source, j, sem, to):
        return pltpu.make_async_remote_copy(
            src_ref=gathered.at[source, j],
            dst_ref=gathered.at[source, j],
            send_sem=sem,
            recv_sem=chain_sem.at[source, j],
            device_id={"scen": to},
            device_id_type=MESH,
        )

    def part_send(q, d):
        to = lax.rem(t + d, n)
        return pltpu.make_async_remote_copy(
            src_ref=parts.at[q, to],
            dst_ref=got_ref.at[t, q],
            send_sem=part_sem.at[q, d - 1],
            recv_sem=got_sem.at[t, q],
            device_id={"tile": to},
            device_id_type=MESH,
        )

    def part_arrival(source, q):
        return pltpu.make_async_remote_copy(
            src_ref=parts.at[q, source],
            dst_ref=got_ref.at[source, q],
            send_sem=part_sem.at[q, 0],
            recv_sem=got_sem.at[source, q],
            device_id={"tile": source},
            device_id_type=MESH,
        )

    def part_keep(q):
        return pltpu.make_async_copy(parts.at[q, t], got_ref.at[t, q], keep_sem.at[q])

    def step_send(d):
        to = lax.rem(z + d, n)
        return pltpu.make_async_remote_copy(
            src_ref=step_box.at[z],
            dst_ref=step_box.at[z],
            send_sem=step_sem.at[d - 1],
            recv_sem=step_got_sem.at[z],
            device_id={"scen": to},
            device_id_type=MESH,
        )

    def step_arrival(d):
        source = lax.rem(z + d, n)
        return pltpu.make_async_remote_copy(
            src_ref=step_box.at[source],
            dst_ref=step_box.at[source],
            send_sem=step_sem.at[d - 1],
            recv_sem=step_got_sem.at[source],
            device_id={"scen": source},
            device_id_type=MESH,
        )

    def gram(source, j):
        q = source * held + j
        block = gathered.at[source, j]
        left = jnp.concatenate(
            [
                block[:, pl.ds(pl.multiple_of((z + a * n) * BW, BW), BW)]
                for a in range(2)
            ],
            axis=1,
        )
        turned = left.T
        for to in range(n):
            right = jnp.concatenate(
                [block[:, (to + b * n) * BW : (to + b * n + 1) * BW] for b in range(2)], axis=1
            )
            parts[q, to] = jnp.dot(turned, right, preferred_element_type=jnp.float32).astype(
                jnp.bfloat16
            )
        for d in range(1, n):
            part_send(q, d).start()
        part_keep(q).start()

    for j in range(held):
        load(j).start()
    barrier = pltpu.get_barrier_semaphore()
    for d in range(1, n):
        pl.semaphore_signal(
            barrier, inc=1, device_id={"scen": lax.rem(z + d, n)}, device_id_type=MESH
        )
        pl.semaphore_signal(
            barrier, inc=1, device_id={"tile": lax.rem(t + d, n)}, device_id_type=MESH
        )
    step_box[z] = step_ref[...].astype(jnp.bfloat16)
    pl.semaphore_wait(barrier, 2 * (n - 1))

    for j in range(held):
        load(j).wait()

        @pl.when(z < n - 1)
        def _():
            hop(z, j, own_sem.at[0, j], z + 1).start()

        @pl.when(z > 0)
        def _():
            hop(z, j, own_sem.at[1, j], z - 1).start()

    for d in range(1, n):
        step_send(d).start()

    @pl.loop(0, held)
    def _(j):
        gram(z, j)

    @pl.loop(0, 2 * held * (n - 1))
    def _(i):
        d = 1 + i // (2 * held)
        j = (i // 2) % held
        way = 1 - 2 * (i % 2)
        source = z - way * d
        onward = z + way

        @pl.when((source >= 0) & (source < n))
        def _():
            hop(source, j, pass_sem.at[source, j], z).wait_recv()

            @pl.when((onward >= 0) & (onward < n))
            def _():
                hop(source, j, pass_sem.at[source, j], onward).start()

            gram(source, j)

    for d in range(1, n):
        step_send(d).wait_send()
        step_arrival(d).wait_recv()
    steps_ref[...] = step_box[...].reshape(steps_ref.shape)

    for j in range(held):

        @pl.when(z < n - 1)
        def _():
            hop(z, j, own_sem.at[0, j], z + 1).wait_send()

        @pl.when(z > 0)
        def _():
            hop(z, j, own_sem.at[1, j], z - 1).wait_send()

    @pl.loop(0, 2 * held * (n - 1))
    def _(i):
        d = 1 + i // (2 * held)
        j = (i // 2) % held
        way = 1 - 2 * (i % 2)
        source = z - way * d
        onward = z + way

        @pl.when((source >= 0) & (source < n) & (onward >= 0) & (onward < n))
        def _():
            hop(source, j, pass_sem.at[source, j], onward).wait_send()

    @pl.loop(0, n * held)
    def _(q):
        part_keep(q).wait()
        for d in range(1, n):
            part_send(q, d).wait_send()
            part_arrival(lax.rem(t + d, n), q).wait_recv()


def exchange(n, scaled, step_dx):
    held, rows, width = scaled.shape
    return pl.pallas_call(
        functools.partial(exchange_kernel, n, held),
        out_shape=(
            jax.ShapeDtypeStruct((n, n * held, 2 * BW, 2 * BW), jnp.bfloat16),
            jax.ShapeDtypeStruct((n * step_dx.shape[0], BW), jnp.bfloat16),
        ),
        in_specs=[pl.BlockSpec(memory_space=pl.ANY), pl.BlockSpec(memory_space=pltpu.VMEM)],
        out_specs=(pl.BlockSpec(memory_space=pl.ANY), pl.BlockSpec(memory_space=pltpu.VMEM)),
        scratch_shapes=[
            pltpu.VMEM((n, held, rows, width), jnp.bfloat16),
            pltpu.VMEM((n * held, n, 2 * BW, 2 * BW), jnp.bfloat16),
            pltpu.VMEM((n,) + step_dx.shape, jnp.bfloat16),
            pltpu.SemaphoreType.DMA((held,)),
            pltpu.SemaphoreType.DMA((2, held)),
            pltpu.SemaphoreType.DMA((n, held)),
            pltpu.SemaphoreType.DMA((n, held)),
            pltpu.SemaphoreType.DMA((n * held, n - 1)),
            pltpu.SemaphoreType.DMA((n, n * held)),
            pltpu.SemaphoreType.DMA((n * held,)),
            pltpu.SemaphoreType.DMA((n - 1,)),
            pltpu.SemaphoreType.DMA((n,)),
        ],
        compiler_params=pltpu.CompilerParams(
            collective_id=0, has_side_effects=True, vmem_limit_bytes=40 * 2**20
        ),
        name="exchange",
    )(scaled, step_dx)


def assemble_kernel(
    n, held, cap, blocks_ref, got_ref, diag_ref, steps_ref, linking_ref, scaling_ref, residual_ref,
    schur_ref, back_ref, box, total, wide, in_sem, out_sem,
):
    z = lax.axis_index("scen")
    t = lax.axis_index("tile")
    half = cap // 2

    def load(a):
        return pltpu.make_async_copy(
            got_ref.at[:, :, pl.ds(a * BW, BW)], box.at[a], in_sem.at[a]
        )

    def store(a):
        rows = pl.ds(a * half * BW, half * BW)
        return pltpu.make_async_copy(total.at[rows], schur_ref.at[rows], out_sem.at[a])

    load(0).start()
    load(1).start()
    on_diagonal = lax.broadcasted_iota(jnp.int32, (BW, BW), 0) == lax.broadcasted_iota(
        jnp.int32, (BW, BW), 1
    )
    wide[...] = steps_ref[...].astype(jnp.float32)
    for a in range(2):

        @pl.loop(0, 4 * half)
        def _(i):
            rows = pl.ds(pl.multiple_of(a * half * BW + i * (BW // 4), BW // 4), BW // 4)
            total[rows, :] = jnp.zeros((BW // 4, cap * BW), jnp.float32)

        @pl.when(z == t)
        def _():
            for r in range(a * half, (a + 1) * half):
                total[r * BW : (r + 1) * BW, r * BW : (r + 1) * BW] = jnp.where(
                    on_diagonal, diag_ref[r : r + 1, :], 0.0
                )

        load(a).wait()

        @pl.loop(0, n * n * held)
        def _(i):
            source, q = i // (n * held), i % (n * held)
            s = ((q // held) * n + source) * held + q % held
            row = lax.rem(blocks_ref[s, z + a * n], cap)
            rows = pl.ds(pl.multiple_of(row * BW, BW), BW)
            for b in range(2):
                col = lax.rem(blocks_ref[s, t + b * n], cap)
                cols = pl.ds(pl.multiple_of(col * BW, BW), BW)
                total[rows, cols] += box[a, source, q, :, b * BW : (b + 1) * BW].astype(jnp.float32)

        store(a).start()
    for j in range(held):
        mine = (z * n + t) * held + j
        picked = jnp.concatenate(
            [wide[pl.ds(blocks_ref[mine, k], 1), :] for k in range(2 * n)], axis=1
        )
        applied = lax.dot_general(
            picked.astype(jnp.bfloat16),
            linking_ref[j],
            (((1,), (1,)), ((), ())),
            preferred_element_type=jnp.float32,
        )
        back_ref[j : j + 1, :] = scaling_ref[j : j + 1, :] * (residual_ref[j : j + 1, :] - applied)
    store(0).wait()
    store(1).wait()


def assemble(n, blocks, got, first_diag, steps, linking, scaling, residual):
    held = linking.shape[0]
    cap = first_diag.shape[0] // BW
    vmem = pl.BlockSpec(memory_space=pltpu.VMEM)
    anywhere = pl.BlockSpec(memory_space=pl.ANY)
    return pl.pallas_call(
        functools.partial(assemble_kernel, n, held, cap),
        out_shape=(
            jax.ShapeDtypeStruct((cap * BW, cap * BW), jnp.float32),
            jax.ShapeDtypeStruct(scaling.shape, jnp.float32),
        ),
        in_specs=[
            pl.BlockSpec(memory_space=pltpu.SMEM), anywhere, vmem, vmem, vmem, vmem, vmem,
        ],
        out_specs=(anywhere, vmem),
        scratch_shapes=[
            pltpu.VMEM((2, n, n * held, BW, 2 * BW), jnp.bfloat16),
            pltpu.VMEM((cap * BW, cap * BW), jnp.float32),
            pltpu.VMEM(steps.shape, jnp.float32),
            pltpu.SemaphoreType.DMA((2,)),
            pltpu.SemaphoreType.DMA((2,)),
        ],
        compiler_params=pltpu.CompilerParams(vmem_limit_bytes=40 * 2**20),
        name="assemble",
    )(blocks, got, first_diag.reshape(cap, BW), steps, linking, scaling, residual)


def on_square(linking, scaling, residual, blocks, step_dx, first_diag):
    n = lax.axis_size("tile")
    scaled = (jnp.sqrt(scaling)[:, :, None] * linking).astype(jnp.bfloat16)
    got, steps = exchange(n, scaled, step_dx)
    return assemble(n, blocks, got, first_diag, steps, linking, scaling, residual)


def solution(mesh):
    in_specs = (
        P(("groups", "scen", "tile"), None, None),
        P(("groups", "scen", "tile"), None),
        P(("groups", "scen", "tile"), None),
        P("groups", None),
        P(("groups", "scen"), None),
        P(("groups", "scen")),
    )
    out_specs = (P(("groups", "scen"), "tile"), P(("groups", "scen", "tile"), None))
    tiles_ax, scen_ax = mesh.shape["tile"], mesh.shape["scen"]
    square = scen_ax == tiles_ax and LIST == 2 * tiles_ax
    return jax.shard_map(
        on_square if square else on_device, mesh=mesh, in_specs=in_specs, out_specs=out_specs, check_vma=False
    )
```

```python
import functools

import jax
import jax.numpy as jnp
from jax import lax
from jax.experimental import pallas as pl
from jax.experimental.pallas import tpu as pltpu
from jax.sharding import PartitionSpec as P

BW = 128
LIST = 8
NBLK = 64


def on_device(linking, scaling, residual, blocks, step_dx, first_diag):
    tiles_ax = lax.axis_size("tile")
    scen_ax = lax.axis_size("scen")
    here_scen = lax.axis_index("scen")
    here_tile = lax.axis_index("tile")
    held_scen = linking.shape[0]
    shard_size = tiles_ax * held_scen
    width_rows = step_dx.shape[0]
    width_cols = NBLK // tiles_ax
    per_group = LIST // tiles_ax
    owners_per = scen_ax // tiles_ax
    cap_owner = min(shard_size, (3 * shard_size + 2 * owners_per - 1) // (2 * owners_per))
    slot_count = per_group * per_group * cap_owner
    target_count = width_rows * width_cols
    own_blocks = lax.dynamic_slice_in_dim(
        blocks, (here_scen * tiles_ax + here_tile) * held_scen, held_scen, 0
    )
    low_step = step_dx.astype(jnp.bfloat16)
    full_step = lax.all_gather(low_step, "scen", axis=0, tiled=True)
    picked = full_step[own_blocks].reshape(held_scen, LIST * BW)
    applied = jnp.einsum("src,sc->sr", linking, picked, preferred_element_type=jnp.float32)
    back_step = scaling * (residual - applied)
    scaled = (jnp.sqrt(scaling)[:, :, None] * linking).astype(jnp.bfloat16)
    gram_full = jnp.einsum("sra,src->sac", scaled, scaled, preferred_element_type=jnp.float32)
    gram_tiles = (
        gram_full.reshape(held_scen, LIST, BW, LIST, BW)
        .transpose(0, 1, 3, 2, 4)
        .astype(jnp.bfloat16)
    )
    outgoing = gram_tiles.reshape(held_scen, LIST, per_group, tiles_ax, BW, BW).transpose(
        3, 0, 2, 1, 4, 5
    )
    incoming = lax.all_to_all(outgoing, "tile", split_axis=0, concat_axis=0, tiled=True)
    flat_tiles = incoming.reshape(shard_size * per_group * LIST, BW, BW)
    shard_blocks = blocks.reshape(scen_ax, shard_size, LIST)

    def route_tiles(block_lists):
        col_blocks = jnp.take(block_lists, jnp.arange(per_group) * tiles_ax + here_tile, axis=1)
        row_block = jnp.broadcast_to(
            block_lists[:, None, :], (shard_size, per_group, LIST)
        ).reshape(-1)
        col_block = jnp.broadcast_to(col_blocks[:, :, None], (shard_size, per_group, LIST)).reshape(
            -1
        )
        owner_idx = row_block // width_rows
        hit_table = (owner_idx[:, None] == jnp.arange(scen_ax)[None, :]).astype(jnp.int32)
        before = jnp.cumsum(hit_table, axis=0) - hit_table
        slot_rank = jnp.sum(before * hit_table, axis=1)
        target = row_block % width_rows * width_cols + col_block % width_cols
        return (owner_idx, slot_rank, target)

    own_lists = lax.dynamic_index_in_dim(shard_blocks, here_scen, 0, keepdims=False)
    send_owner, send_rank, unused = route_tiles(own_lists)
    outbox = (
        jnp.zeros((scen_ax, slot_count, BW, BW), jnp.bfloat16)
        .at[send_owner, send_rank]
        .set(flat_tiles)
    )
    received = lax.all_to_all(outbox, "scen", split_axis=0, concat_axis=0, tiled=True)
    all_owner, all_rank, all_target = jax.vmap(route_tiles)(shard_blocks)
    is_mine = all_owner == here_scen
    slot_id = jnp.arange(scen_ax)[:, None] * slot_count + all_rank
    pick_target = (
        (all_target[:, :, None] == jnp.arange(target_count)[None, None, :]) & is_mine[:, :, None]
    ).astype(jnp.float32)
    pick_slot = (slot_id[:, :, None] == jnp.arange(scen_ax * slot_count)[None, None, :]).astype(
        jnp.float32
    )
    select = jnp.einsum("pnt,pnz->tz", pick_target, pick_slot).astype(jnp.bfloat16)
    summed = jnp.dot(
        select, received.reshape(scen_ax * slot_count, BW * BW), preferred_element_type=jnp.float32
    )
    schur_block = (
        summed.reshape(width_rows, width_cols, BW, BW)
        .transpose(0, 2, 1, 3)
        .reshape(width_rows * BW, width_cols * BW)
    )
    rows_global = here_scen * (width_rows * BW) + jnp.arange(width_rows * BW)
    cols_global = here_tile * (width_cols * BW) + jnp.arange(width_cols * BW)
    schur_block = schur_block + jnp.where(
        rows_global[:, None] == cols_global[None, :], first_diag[:, None], 0.0
    )
    return (schur_block, back_step)


MESH = pl.DeviceIdType.MESH
PACK = BW + 16


def pair_masks():
    rows = lax.broadcasted_iota(jnp.int32, (BW, BW), 0)
    cols = lax.broadcasted_iota(jnp.int32, (BW, BW), 1)
    return rows > cols, rows == cols, rows < cols


def exchange_kernel(
    n, held, linking_ref, scaling_ref, step_ref, got_ref, steps_ref,
    gathered, parts, end_parts, step_box,
    own_sem, pass_sem, chain_sem, end_sem, end_got_sem, part_sem, got_sem, keep_sem,
    step_sem, step_got_sem,
):
    z = lax.axis_index("scen")
    t = lax.axis_index("tile")
    side = z // (n // 2)
    end = side * (n - 1)
    turn = 1 - 2 * side
    inner = (z > 0) & (z < n - 1)
    peers = (lax.rem(t + 2, n), n - 1 - t, t + 1 - 2 * lax.rem(t, 2))
    below, level, above = pair_masks()

    def is_inner(place):
        return (place > 0) & (place < n - 1)

    def hop(source, j, sem, to):
        return pltpu.make_async_remote_copy(
            src_ref=gathered.at[source, j],
            dst_ref=gathered.at[source, j],
            send_sem=sem,
            recv_sem=chain_sem.at[source, j],
            device_id={"scen": to},
            device_id_type=MESH,
        )

    def by_size(packed, act):
        @pl.when(packed)
        def _():
            act(PACK)

        @pl.when(jnp.logical_not(packed))
        def _():
            act(2 * BW)

    def end_send(q, to, size):
        return pltpu.make_async_remote_copy(
            src_ref=end_parts.at[q, to, pl.ds(0, size)],
            dst_ref=parts.at[q, to, pl.ds(0, size)],
            send_sem=end_sem.at[q, to],
            recv_sem=end_got_sem.at[q, to],
            device_id={"scen": end},
            device_id_type=MESH,
        )

    def part_send(q, to, size):
        return pltpu.make_async_remote_copy(
            src_ref=parts.at[q, to, pl.ds(0, size)],
            dst_ref=got_ref.at[t, q, pl.ds(0, size)],
            send_sem=part_sem.at[q, to],
            recv_sem=got_sem.at[t, q],
            device_id={"tile": to},
            device_id_type=MESH,
        )

    def part_arrival(source, q, size):
        return pltpu.make_async_remote_copy(
            src_ref=parts.at[q, source, pl.ds(0, size)],
            dst_ref=got_ref.at[source, q, pl.ds(0, size)],
            send_sem=part_sem.at[q, source],
            recv_sem=got_sem.at[source, q],
            device_id={"tile": source},
            device_id_type=MESH,
        )

    def part_keep(q, size):
        return pltpu.make_async_copy(
            parts.at[q, t, pl.ds(0, size)], got_ref.at[t, q, pl.ds(0, size)], keep_sem.at[q]
        )

    def step_copy(place, to, d):
        return pltpu.make_async_remote_copy(
            src_ref=step_box.at[place],
            dst_ref=step_box.at[place],
            send_sem=step_sem.at[d - 1],
            recv_sem=step_got_sem.at[place],
            device_id={"scen": to},
            device_id_type=MESH,
        )

    def gram(dest, source, j, out):
        q = source * held + j
        block = gathered.at[source, j]
        left = jnp.concatenate(
            [block[:, pl.ds(pl.multiple_of((dest + a * n) * BW, BW), BW)] for a in range(2)],
            axis=1,
        )
        turned = left.T
        for to in range(n):
            right = jnp.concatenate(
                [block[:, (to + b * n) * BW : (to + b * n + 1) * BW] for b in range(2)], axis=1
            )
            tiles = jnp.dot(turned, right, preferred_element_type=jnp.float32)

            @pl.when(dest != to)
            def _():
                out[q, to] = tiles.astype(jnp.bfloat16)

            @pl.when(dest == to)
            def _():
                first, cross, second = tiles[:BW, :BW], tiles[:BW, BW:], tiles[BW:, BW:]
                out[q, to, :BW, :BW] = jnp.where(above, second, first).astype(jnp.bfloat16)
                out[q, to, :BW, BW:] = cross.astype(jnp.bfloat16)
                line = jnp.sum(jnp.where(level, second, 0.0), axis=0, keepdims=True)
                out[q, to, BW:PACK, :BW] = jnp.broadcast_to(line, (PACK - BW, BW)).astype(
                    jnp.bfloat16
                )

    def unpack(source, q):
        mixed = got_ref[source, q, :BW, :BW].astype(jnp.float32)
        cross = got_ref[source, q, :BW, BW:].astype(jnp.float32)
        line = got_ref[source, q, BW:PACK, :BW].astype(jnp.float32)[:1]
        flipped = mixed.T
        first = jnp.where(above, flipped, mixed)
        second = jnp.where(above, mixed, jnp.where(below, flipped, line))
        got_ref[source, q, :BW, :BW] = first.astype(jnp.bfloat16)
        got_ref[source, q, BW:, :BW] = cross.T.astype(jnp.bfloat16)
        got_ref[source, q, BW:, BW:] = second.astype(jnp.bfloat16)

    def to_end(source, j):
        q = source * held + j
        gram(end, source, j, end_parts)
        for to in peers + (t,):
            by_size(to == end, lambda size: end_send(q, to, size).start())

    def to_plane(source, j):
        q = source * held + j
        gram(z, source, j, parts)
        for to in peers:
            by_size(to == z, lambda size: part_send(q, to, size).start())
        by_size(t == z, lambda size: part_keep(q, size).start())

    barrier = pltpu.get_barrier_semaphore()
    for d in range(1, n):
        pl.semaphore_signal(
            barrier, inc=1, device_id={"scen": lax.rem(z + d, n)}, device_id_type=MESH
        )
        pl.semaphore_signal(
            barrier, inc=1, device_id={"tile": lax.rem(t + d, n)}, device_id_type=MESH
        )
    step_box[z] = step_ref[...].astype(jnp.bfloat16)
    rows = linking_ref.shape[1]
    diagonal = lax.broadcasted_iota(jnp.int32, (rows, rows), 0) == lax.broadcasted_iota(
        jnp.int32, (rows, rows), 1
    )
    for j in range(held):
        root = jnp.sqrt(scaling_ref[j : j + 1, :])
        column = jnp.sum(jnp.where(diagonal, root, 0.0), axis=1, keepdims=True)
        gathered[z, j] = (column * linking_ref[j].astype(jnp.float32)).astype(jnp.bfloat16)
    pl.semaphore_wait(barrier, 2 * (n - 1))

    @pl.loop(0, held)
    def _(j):
        for way in (1, -1):

            @pl.when(is_inner(z + way))
            def _():
                hop(z, j, own_sem.at[(1 - way) // 2, j], z + way).start()

        @pl.when(inner)
        def _():
            to_end(z, j)

    for d in range(1, n):
        step_copy(z, lax.rem(z + d, n), d).start()

    @pl.loop(0, held)
    def _(j):
        to_plane(z, j)

    @pl.when(inner)
    def _():
        @pl.loop(0, 2 * held * (n - 2))
        def _(i):
            d = 1 + i // (2 * held)
            j = (i // 2) % held
            way = 1 - 2 * (i % 2)
            source = z - way * d
            onward = z + way

            @pl.when((source >= 0) & (source < n))
            def _():
                hop(source, j, pass_sem.at[source, j], z).wait_recv()

                @pl.when(is_inner(onward))
                def _():
                    hop(source, j, pass_sem.at[source, j], onward).start()

                @pl.when(jnp.logical_not(is_inner(onward)))
                def _():
                    to_end(source, j)

                to_plane(source, j)

    @pl.when(jnp.logical_not(inner))
    def _():
        @pl.loop(0, held * (n - 1))
        def _(i):
            q = (z + turn * (1 + i // held)) * held + i % held
            for to in peers:
                by_size(to == z, lambda size: end_send(q, to, size).wait_recv())
                by_size(to == z, lambda size: part_send(q, to, size).start())
            by_size(t == z, lambda size: end_send(q, t, size).wait_recv())
            by_size(t == z, lambda size: part_keep(q, size).start())

    for d in range(1, n):
        step_copy(z, lax.rem(z + d, n), d).wait_send()
        source = lax.rem(z + d, n)
        step_copy(source, source, d).wait_recv()
    steps_ref[...] = step_box[...].reshape(steps_ref.shape)

    @pl.loop(0, held)
    def _(j):
        for way in (1, -1):

            @pl.when(is_inner(z + way))
            def _():
                hop(z, j, own_sem.at[(1 - way) // 2, j], z + way).wait_send()

    @pl.when(inner)
    def _():
        @pl.loop(0, held)
        def _(j):
            hop(end, j, pass_sem.at[end, j], z + turn).wait_send()

        @pl.loop(0, held * (n - 1))
        def _(i):
            q = (end + turn * (1 + i // held)) * held + i % held
            for to in range(n):
                by_size(to == end, lambda size: end_send(q, to, size).wait_send())

    @pl.loop(0, n * held)
    def _(i):
        q = lax.rem(z + turn * (i // held) + n, n) * held + i % held
        by_size(t == z, lambda size: part_keep(q, size).wait())
        for to in peers:
            by_size(t == z, lambda size: part_arrival(to, q, size).wait_recv())

        @pl.when(t == z)
        def _():
            for source in range(n):
                unpack(source, q)

        for to in peers:
            by_size(to == z, lambda size: part_send(q, to, size).wait_send())


def exchange(n, linking, scaling, step_dx):
    held, rows, width = linking.shape
    vmem = pl.BlockSpec(memory_space=pltpu.VMEM)
    return pl.pallas_call(
        functools.partial(exchange_kernel, n, held),
        out_shape=(
            jax.ShapeDtypeStruct((n, n * held, 2 * BW, 2 * BW), jnp.bfloat16),
            jax.ShapeDtypeStruct((n * step_dx.shape[0], BW), jnp.bfloat16),
        ),
        in_specs=[vmem] * 3,
        out_specs=(vmem, vmem),
        scratch_shapes=[
            pltpu.VMEM((n, held, rows, width), jnp.bfloat16),
            pltpu.VMEM((n * held, n, 2 * BW, 2 * BW), jnp.bfloat16),
            pltpu.VMEM((n * held, n, 2 * BW, 2 * BW), jnp.bfloat16),
            pltpu.VMEM((n,) + step_dx.shape, jnp.bfloat16),
            pltpu.SemaphoreType.DMA((2, held)),
            pltpu.SemaphoreType.DMA((n, held)),
            pltpu.SemaphoreType.DMA((n, held)),
            pltpu.SemaphoreType.DMA((n * held, n)),
            pltpu.SemaphoreType.DMA((n * held, n)),
            pltpu.SemaphoreType.DMA((n * held, n)),
            pltpu.SemaphoreType.DMA((n, n * held)),
            pltpu.SemaphoreType.DMA((n * held,)),
            pltpu.SemaphoreType.DMA((n - 1,)),
            pltpu.SemaphoreType.DMA((n,)),
        ],
        compiler_params=pltpu.CompilerParams(
            collective_id=0, has_side_effects=True, vmem_limit_bytes=36 * 2**20
        ),
        name="exchange",
    )(linking, scaling, step_dx)


def assemble_kernel(
    n, held, cap, lists_ref, got_ref, diag_ref, steps_ref, linking_ref, scaling_ref, residual_ref,
    schur_ref, back_ref, total, wide, out_sem,
):
    z = lax.axis_index("scen")
    t = lax.axis_index("tile")
    half = cap // 2
    span = half * BW

    def store(a, b):
        place = (pl.ds(a * span, span), pl.ds(b * span, span))
        return pltpu.make_async_copy(total.at[place], schur_ref.at[place], out_sem.at[a, b])

    level = pair_masks()[1]
    for a in range(2):
        for b in range(2):

            @pl.loop(0, 2 * half)
            def _(i):
                rows = pl.ds(pl.multiple_of(a * span + i * (BW // 2), BW // 2), BW // 2)
                total[rows, b * span : (b + 1) * span] = jnp.zeros((BW // 2, span), jnp.float32)

            if a == b:

                @pl.when(z == t)
                def _():
                    for r in range(a * half, (a + 1) * half):
                        total[r * BW : (r + 1) * BW, r * BW : (r + 1) * BW] = jnp.where(
                            level, diag_ref[r : r + 1, :], 0.0
                        )

            @pl.loop(0, n * n * held, unroll=4)
            def _(i):
                source, q = i // (n * held), i % (n * held)
                s = ((q // held) * n + source) * held + q % held
                row = lax.rem(lists_ref[z + a * n, s], cap)
                col = lax.rem(lists_ref[t + b * n, s], cap)
                rows = pl.ds(pl.multiple_of(row * BW, BW), BW)
                cols = pl.ds(pl.multiple_of(col * BW, BW), BW)
                total[rows, cols] += got_ref[
                    source, q, a * BW : (a + 1) * BW, b * BW : (b + 1) * BW
                ].astype(jnp.float32)

            store(a, b).start()
    wide[...] = steps_ref[...].astype(jnp.float32)
    for j in range(held):
        mine = (z * n + t) * held + j
        picked = jnp.concatenate(
            [wide[pl.ds(lists_ref[k, mine], 1), :] for k in range(2 * n)], axis=1
        )
        applied = lax.dot_general(
            picked.astype(jnp.bfloat16),
            linking_ref[j],
            (((1,), (1,)), ((), ())),
            preferred_element_type=jnp.float32,
        )
        back_ref[j : j + 1, :] = scaling_ref[j : j + 1, :] * (residual_ref[j : j + 1, :] - applied)
    for a in range(2):
        for b in range(2):
            store(a, b).wait()


def assemble(n, lists, got, first_diag, steps, linking, scaling, residual):
    held = linking.shape[0]
    cap = first_diag.shape[0] // BW
    vmem = pl.BlockSpec(memory_space=pltpu.VMEM)
    return pl.pallas_call(
        functools.partial(assemble_kernel, n, held, cap),
        out_shape=(
            jax.ShapeDtypeStruct((cap * BW, cap * BW), jnp.float32),
            jax.ShapeDtypeStruct(scaling.shape, jnp.float32),
        ),
        in_specs=[pl.BlockSpec(memory_space=pltpu.SMEM)] + [vmem] * 6,
        out_specs=(pl.BlockSpec(memory_space=pl.ANY), vmem),
        scratch_shapes=[
            pltpu.VMEM((cap * BW, cap * BW), jnp.float32),
            pltpu.VMEM(steps.shape, jnp.float32),
            pltpu.SemaphoreType.DMA((2, 2)),
        ],
        compiler_params=pltpu.CompilerParams(vmem_limit_bytes=36 * 2**20),
        name="assemble",
    )(lists, got, first_diag.reshape(cap, BW), steps, linking, scaling, residual)


def on_square(linking, scaling, residual, blocks, step_dx, first_diag):
    n = lax.axis_size("tile")
    got, steps = exchange(n, linking, scaling, step_dx)
    return assemble(n, blocks.T, got, first_diag, steps, linking, scaling, residual)


def solution(mesh):
    in_specs = (
        P(("groups", "scen", "tile"), None, None),
        P(("groups", "scen", "tile"), None),
        P(("groups", "scen", "tile"), None),
        P("groups", None),
        P(("groups", "scen"), None),
        P(("groups", "scen")),
    )
    out_specs = (P(("groups", "scen"), "tile"), P(("groups", "scen", "tile"), None))
    tiles_ax, scen_ax = mesh.shape["tile"], mesh.shape["scen"]
    square = scen_ax == tiles_ax and LIST == 2 * tiles_ax
    return jax.shard_map(
        on_square if square else on_device, mesh=mesh, in_specs=in_specs, out_specs=out_specs, check_vma=False
    )
```

```python
import functools

import jax
import jax.numpy as jnp
from jax import lax
from jax.experimental import pallas as pl
from jax.experimental.pallas import tpu as pltpu
from jax.sharding import PartitionSpec as P

BW = 128
LIST = 8
NBLK = 64


def on_device(linking, scaling, residual, blocks, step_dx, first_diag):
    tiles_ax = lax.axis_size("tile")
    scen_ax = lax.axis_size("scen")
    here_scen = lax.axis_index("scen")
    here_tile = lax.axis_index("tile")
    held_scen = linking.shape[0]
    shard_size = tiles_ax * held_scen
    width_rows = step_dx.shape[0]
    width_cols = NBLK // tiles_ax
    per_group = LIST // tiles_ax
    owners_per = scen_ax // tiles_ax
    cap_owner = min(shard_size, (3 * shard_size + 2 * owners_per - 1) // (2 * owners_per))
    slot_count = per_group * per_group * cap_owner
    target_count = width_rows * width_cols
    own_blocks = lax.dynamic_slice_in_dim(
        blocks, (here_scen * tiles_ax + here_tile) * held_scen, held_scen, 0
    )
    low_step = step_dx.astype(jnp.bfloat16)
    full_step = lax.all_gather(low_step, "scen", axis=0, tiled=True)
    picked = full_step[own_blocks].reshape(held_scen, LIST * BW)
    applied = jnp.einsum("src,sc->sr", linking, picked, preferred_element_type=jnp.float32)
    back_step = scaling * (residual - applied)
    scaled = (jnp.sqrt(scaling)[:, :, None] * linking).astype(jnp.bfloat16)
    gram_full = jnp.einsum("sra,src->sac", scaled, scaled, preferred_element_type=jnp.float32)
    gram_tiles = (
        gram_full.reshape(held_scen, LIST, BW, LIST, BW)
        .transpose(0, 1, 3, 2, 4)
        .astype(jnp.bfloat16)
    )
    outgoing = gram_tiles.reshape(held_scen, LIST, per_group, tiles_ax, BW, BW).transpose(
        3, 0, 2, 1, 4, 5
    )
    incoming = lax.all_to_all(outgoing, "tile", split_axis=0, concat_axis=0, tiled=True)
    flat_tiles = incoming.reshape(shard_size * per_group * LIST, BW, BW)
    shard_blocks = blocks.reshape(scen_ax, shard_size, LIST)

    def route_tiles(block_lists):
        col_blocks = jnp.take(block_lists, jnp.arange(per_group) * tiles_ax + here_tile, axis=1)
        row_block = jnp.broadcast_to(
            block_lists[:, None, :], (shard_size, per_group, LIST)
        ).reshape(-1)
        col_block = jnp.broadcast_to(col_blocks[:, :, None], (shard_size, per_group, LIST)).reshape(
            -1
        )
        owner_idx = row_block // width_rows
        hit_table = (owner_idx[:, None] == jnp.arange(scen_ax)[None, :]).astype(jnp.int32)
        before = jnp.cumsum(hit_table, axis=0) - hit_table
        slot_rank = jnp.sum(before * hit_table, axis=1)
        target = row_block % width_rows * width_cols + col_block % width_cols
        return (owner_idx, slot_rank, target)

    own_lists = lax.dynamic_index_in_dim(shard_blocks, here_scen, 0, keepdims=False)
    send_owner, send_rank, unused = route_tiles(own_lists)
    outbox = (
        jnp.zeros((scen_ax, slot_count, BW, BW), jnp.bfloat16)
        .at[send_owner, send_rank]
        .set(flat_tiles)
    )
    received = lax.all_to_all(outbox, "scen", split_axis=0, concat_axis=0, tiled=True)
    all_owner, all_rank, all_target = jax.vmap(route_tiles)(shard_blocks)
    is_mine = all_owner == here_scen
    slot_id = jnp.arange(scen_ax)[:, None] * slot_count + all_rank
    pick_target = (
        (all_target[:, :, None] == jnp.arange(target_count)[None, None, :]) & is_mine[:, :, None]
    ).astype(jnp.float32)
    pick_slot = (slot_id[:, :, None] == jnp.arange(scen_ax * slot_count)[None, None, :]).astype(
        jnp.float32
    )
    select = jnp.einsum("pnt,pnz->tz", pick_target, pick_slot).astype(jnp.bfloat16)
    summed = jnp.dot(
        select, received.reshape(scen_ax * slot_count, BW * BW), preferred_element_type=jnp.float32
    )
    schur_block = (
        summed.reshape(width_rows, width_cols, BW, BW)
        .transpose(0, 2, 1, 3)
        .reshape(width_rows * BW, width_cols * BW)
    )
    rows_global = here_scen * (width_rows * BW) + jnp.arange(width_rows * BW)
    cols_global = here_tile * (width_cols * BW) + jnp.arange(width_cols * BW)
    schur_block = schur_block + jnp.where(
        rows_global[:, None] == cols_global[None, :], first_diag[:, None], 0.0
    )
    return (schur_block, back_step)


MESH = pl.DeviceIdType.MESH
PACK = BW + 16


def pair_masks():
    rows = lax.broadcasted_iota(jnp.int32, (BW, BW), 0)
    cols = lax.broadcasted_iota(jnp.int32, (BW, BW), 1)
    return rows > cols, rows == cols, rows < cols


def exchange_kernel(
    n, held, scaled_ref, step_ref, got_ref, steps_ref,
    gathered, parts, end_parts, step_box,
    load_sem, own_sem, pass_sem, chain_sem, end_sem, end_got_sem, part_sem, got_sem, keep_sem,
    step_sem, step_got_sem,
):
    z = lax.axis_index("scen")
    t = lax.axis_index("tile")
    side = z // (n // 2)
    end = side * (n - 1)
    turn = 1 - 2 * side
    inner = (z > 0) & (z < n - 1)
    peers = (lax.rem(t + 2, n), n - 1 - t, t + 1 - 2 * lax.rem(t, 2))
    below, level, above = pair_masks()

    def is_inner(place):
        return (place > 0) & (place < n - 1)

    def hop(source, j, sem, to):
        return pltpu.make_async_remote_copy(
            src_ref=gathered.at[source, j],
            dst_ref=gathered.at[source, j],
            send_sem=sem,
            recv_sem=chain_sem.at[source, j],
            device_id={"scen": to},
            device_id_type=MESH,
        )

    def by_size(packed, act):
        @pl.when(packed)
        def _():
            act(PACK)

        @pl.when(jnp.logical_not(packed))
        def _():
            act(2 * BW)

    def end_send(q, to, size):
        return pltpu.make_async_remote_copy(
            src_ref=end_parts.at[q, to, pl.ds(0, size)],
            dst_ref=parts.at[q, to, pl.ds(0, size)],
            send_sem=end_sem.at[q, to],
            recv_sem=end_got_sem.at[q, to],
            device_id={"scen": end},
            device_id_type=MESH,
        )

    def part_send(q, to, size):
        return pltpu.make_async_remote_copy(
            src_ref=parts.at[q, to, pl.ds(0, size)],
            dst_ref=got_ref.at[t, q, pl.ds(0, size)],
            send_sem=part_sem.at[q, to],
            recv_sem=got_sem.at[t, q],
            device_id={"tile": to},
            device_id_type=MESH,
        )

    def part_arrival(source, q, size):
        return pltpu.make_async_remote_copy(
            src_ref=parts.at[q, source, pl.ds(0, size)],
            dst_ref=got_ref.at[source, q, pl.ds(0, size)],
            send_sem=part_sem.at[q, source],
            recv_sem=got_sem.at[source, q],
            device_id={"tile": source},
            device_id_type=MESH,
        )

    def part_keep(q, size):
        return pltpu.make_async_copy(
            parts.at[q, t, pl.ds(0, size)], got_ref.at[t, q, pl.ds(0, size)], keep_sem.at[q]
        )

    def step_copy(place, to, d):
        return pltpu.make_async_remote_copy(
            src_ref=step_box.at[place],
            dst_ref=step_box.at[place],
            send_sem=step_sem.at[d - 1],
            recv_sem=step_got_sem.at[place],
            device_id={"scen": to},
            device_id_type=MESH,
        )

    def gram(dest, source, j, out, send):
        q = source * held + j
        block = gathered.at[source, j]
        left = jnp.concatenate(
            [block[:, pl.ds(pl.multiple_of((dest + a * n) * BW, BW), BW)] for a in range(2)],
            axis=1,
        )
        turned = left.T
        for to in peers + (t,):
            right = jnp.concatenate(
                [
                    block[:, pl.ds(pl.multiple_of((to + b * n) * BW, BW), BW)]
                    for b in range(2)
                ],
                axis=1,
            )
            tiles = jnp.dot(turned, right, preferred_element_type=jnp.float32)

            @pl.when(dest != to)
            def _():
                out[q, to] = tiles.astype(jnp.bfloat16)

            @pl.when(dest == to)
            def _():
                first, cross, second = tiles[:BW, :BW], tiles[:BW, BW:], tiles[BW:, BW:]
                out[q, to, :BW, :BW] = jnp.where(above, second, first).astype(jnp.bfloat16)
                out[q, to, :BW, BW:] = cross.astype(jnp.bfloat16)
                line = jnp.sum(jnp.where(level, second, 0.0), axis=0, keepdims=True)
                out[q, to, BW:PACK, :BW] = jnp.broadcast_to(line, (PACK - BW, BW)).astype(
                    jnp.bfloat16
                )

            send(q, to)

    def unpack(source, q):
        mixed = got_ref[source, q, :BW, :BW].astype(jnp.float32)
        cross = got_ref[source, q, :BW, BW:].astype(jnp.float32)
        line = got_ref[source, q, BW:PACK, :BW].astype(jnp.float32)[:1]
        flipped = mixed.T
        first = jnp.where(above, flipped, mixed)
        second = jnp.where(above, mixed, jnp.where(below, flipped, line))
        got_ref[source, q, :BW, :BW] = first.astype(jnp.bfloat16)
        got_ref[source, q, BW:, :BW] = cross.T.astype(jnp.bfloat16)
        got_ref[source, q, BW:, BW:] = second.astype(jnp.bfloat16)

    def to_end(source, j):
        def send(q, to):
            by_size(to == end, lambda size: end_send(q, to, size).start())

        gram(end, source, j, end_parts, send)

    def pass_on(q, to):
        if to is t:
            by_size(t == z, lambda size: part_keep(q, size).start())
        else:
            by_size(to == z, lambda size: part_send(q, to, size).start())

    def to_plane(source, j):
        gram(z, source, j, parts, pass_on)

    def finish(p):
        q = lax.rem(z + turn * (p // held) + n, n) * held + p % held
        by_size(t == z, lambda size: part_keep(q, size).wait())
        for to in peers:
            by_size(t == z, lambda size: part_arrival(to, q, size).wait_recv())

        @pl.when(t == z)
        def _():
            for source in range(n):
                unpack(source, q)

    loads = [
        pltpu.make_async_copy(scaled_ref.at[j], gathered.at[z, j], load_sem.at[j])
        for j in range(held)
    ]
    for load in loads:
        load.start()
    barrier = pltpu.get_barrier_semaphore()
    for d in range(1, n):
        pl.semaphore_signal(
            barrier, inc=1, device_id={"scen": lax.rem(z + d, n)}, device_id_type=MESH
        )
        pl.semaphore_signal(
            barrier, inc=1, device_id={"tile": lax.rem(t + d, n)}, device_id_type=MESH
        )
    step_box[z] = step_ref[...].astype(jnp.bfloat16)
    for load in loads:
        load.wait()
    pl.semaphore_wait(barrier, 2 * (n - 1))

    @pl.loop(0, held)
    def _(j):
        for way in (1, -1):

            @pl.when(is_inner(z + way))
            def _():
                hop(z, j, own_sem.at[(1 - way) // 2, j], z + way).start()

        @pl.when(inner)
        def _():
            to_end(z, j)

    for d in range(1, n):
        step_copy(z, lax.rem(z + d, n), d).start()

    @pl.loop(0, held)
    def _(j):
        to_plane(z, j)

    @pl.when(inner)
    def _():
        @pl.loop(0, 2 * held * (n - 2))
        def _(i):
            d = 1 + i // (2 * held)
            j = (i // 2) % held
            way = 1 - 2 * (i % 2)
            source = z - way * d
            onward = z + way

            @pl.when((source >= 0) & (source < n))
            def _():
                hop(source, j, pass_sem.at[source, j], z).wait_recv()

                @pl.when(is_inner(onward))
                def _():
                    hop(source, j, pass_sem.at[source, j], onward).start()

                @pl.when(jnp.logical_not(is_inner(onward)))
                def _():
                    to_end(source, j)

                to_plane(source, j)

    @pl.when(jnp.logical_not(inner))
    def _():
        @pl.loop(0, held * (n - 1))
        def _(i):
            q = (z + turn * (1 + i // held)) * held + i % held
            for to in peers + (t,):
                by_size(to == z, lambda size: end_send(q, to, size).wait_recv())
                pass_on(q, to)
            finish(i)

    for d in range(1, n):
        step_copy(z, lax.rem(z + d, n), d).wait_send()
        source = lax.rem(z + d, n)
        step_copy(source, source, d).wait_recv()
    steps_ref[...] = step_box[...].reshape(steps_ref.shape)

    @pl.when(inner)
    def _():
        @pl.loop(0, held * (n - 1))
        def _(p):
            finish(p)

    @pl.loop(held * (n - 1), held * n)
    def _(p):
        finish(p)

    @pl.loop(0, held)
    def _(j):
        for way in (1, -1):

            @pl.when(is_inner(z + way))
            def _():
                hop(z, j, own_sem.at[(1 - way) // 2, j], z + way).wait_send()

    @pl.when(inner)
    def _():
        @pl.loop(0, held)
        def _(j):
            hop(end, j, pass_sem.at[end, j], z + turn).wait_send()

        @pl.loop(0, held * (n - 1))
        def _(i):
            q = (end + turn * (1 + i // held)) * held + i % held
            for to in range(n):
                by_size(to == end, lambda size: end_send(q, to, size).wait_send())

    @pl.loop(0, n * held)
    def _(q):
        for to in peers:
            by_size(to == z, lambda size: part_send(q, to, size).wait_send())


def exchange(n, scaled, step_dx):
    held, rows, width = scaled.shape
    vmem = pl.BlockSpec(memory_space=pltpu.VMEM)
    return pl.pallas_call(
        functools.partial(exchange_kernel, n, held),
        out_shape=(
            jax.ShapeDtypeStruct((n, n * held, 2 * BW, 2 * BW), jnp.bfloat16),
            jax.ShapeDtypeStruct((n * step_dx.shape[0], BW), jnp.bfloat16),
        ),
        in_specs=[pl.BlockSpec(memory_space=pl.ANY), vmem],
        out_specs=(vmem, vmem),
        scratch_shapes=[
            pltpu.VMEM((n, held, rows, width), jnp.bfloat16),
            pltpu.VMEM((n * held, n, 2 * BW, 2 * BW), jnp.bfloat16),
            pltpu.VMEM((n * held, n, 2 * BW, 2 * BW), jnp.bfloat16),
            pltpu.VMEM((n,) + step_dx.shape, jnp.bfloat16),
            pltpu.SemaphoreType.DMA((held,)),
            pltpu.SemaphoreType.DMA((2, held)),
            pltpu.SemaphoreType.DMA((n, held)),
            pltpu.SemaphoreType.DMA((n, held)),
            pltpu.SemaphoreType.DMA((n * held, n)),
            pltpu.SemaphoreType.DMA((n * held, n)),
            pltpu.SemaphoreType.DMA((n * held, n)),
            pltpu.SemaphoreType.DMA((n, n * held)),
            pltpu.SemaphoreType.DMA((n * held,)),
            pltpu.SemaphoreType.DMA((n - 1,)),
            pltpu.SemaphoreType.DMA((n,)),
        ],
        compiler_params=pltpu.CompilerParams(
            collective_id=0, has_side_effects=True, vmem_limit_bytes=40 * 2**20
        ),
        cost_estimate=pl.CostEstimate(
            flops=60_000_000_000, bytes_accessed=60_000_000_000 // 400, transcendentals=0
        ),
        name="exchange",
    )(scaled, step_dx)


def assemble_kernel(
    n, held, cap, lists_hbm, diag_hbm, linking_hbm, scaling_hbm, residual_hbm, got_ref, steps_ref,
    schur_ref, back_ref, total, lists_ref, diag_ref, linking_ref, scaling_ref, residual_ref, wide,
    load_sem, out_sem,
):
    z = lax.axis_index("scen")
    t = lax.axis_index("tile")
    span = cap // 2 * BW

    def store(a):
        rows = pl.ds(a * span, span)
        return pltpu.make_async_copy(total.at[rows], schur_ref.at[rows], out_sem.at[a])

    pairs = (
        (lists_hbm, lists_ref), (diag_hbm, diag_ref), (linking_hbm, linking_ref),
        (scaling_hbm, scaling_ref), (residual_hbm, residual_ref),
    )
    loads = [
        pltpu.make_async_copy(far, near, load_sem.at[k]) for k, (far, near) in enumerate(pairs)
    ]
    for load in loads:
        load.start()
    wide[...] = steps_ref[...].astype(jnp.float32)
    level = pair_masks()[1]
    for a in range(2):

        @pl.loop(0, span // 32)
        def _(i):
            rows = pl.ds(pl.multiple_of(a * span + i * 32, 32), 32)
            total[rows, :] = jnp.zeros((32, cap * BW), jnp.float32)

        if a == 0:
            loads[0].wait()
            loads[1].wait()

        @pl.when(z == t)
        def _():
            for r in range(a * cap // 2, (a + 1) * cap // 2):
                total[r * BW : (r + 1) * BW, r * BW : (r + 1) * BW] = jnp.where(
                    level, diag_ref[r : r + 1, :], 0.0
                )

        @pl.loop(0, n * n * held, unroll=4)
        def _(i):
            source, q = i // (n * held), i % (n * held)
            s = ((q // held) * n + source) * held + q % held
            row = lists_ref[z + a * n, s] - z * cap
            places, sums = [], []
            for b in range(2):
                col = lists_ref[t + b * n, s] - t * cap
                place = (
                    pl.ds(pl.multiple_of(row * BW, BW), BW),
                    pl.ds(pl.multiple_of(col * BW, BW), BW),
                )
                tile = got_ref[source, q, a * BW : (a + 1) * BW, b * BW : (b + 1) * BW]
                places.append(place)
                sums.append(total[place] + tile.astype(jnp.float32))
            for place, value in zip(places, sums):
                total[place] = value

        store(a).start()
    for load in loads[2:]:
        load.wait()
    for j in range(held):
        mine = (z * n + t) * held + j
        picked = jnp.concatenate(
            [wide[pl.ds(lists_ref[k, mine], 1), :] for k in range(2 * n)], axis=1
        )
        applied = lax.dot_general(
            picked.astype(jnp.bfloat16),
            linking_ref[j],
            (((1,), (1,)), ((), ())),
            preferred_element_type=jnp.float32,
        )
        back_ref[j : j + 1, :] = scaling_ref[j : j + 1, :] * (residual_ref[j : j + 1, :] - applied)
    store(0).wait()
    store(1).wait()


def assemble(n, lists, diag, linking, scaling, residual, got, steps):
    held = linking.shape[0]
    cap = diag.shape[0]
    vmem = pl.BlockSpec(memory_space=pltpu.VMEM)
    hbm = pl.BlockSpec(memory_space=pltpu.HBM)
    return pl.pallas_call(
        functools.partial(assemble_kernel, n, held, cap),
        out_shape=(
            jax.ShapeDtypeStruct((cap * BW, cap * BW), jnp.float32),
            jax.ShapeDtypeStruct(scaling.shape, jnp.float32),
        ),
        in_specs=[hbm] * 5 + [vmem] * 2,
        out_specs=(hbm, vmem),
        scratch_shapes=[
            pltpu.VMEM((cap * BW, cap * BW), jnp.float32),
            pltpu.SMEM(lists.shape, jnp.int32),
            pltpu.VMEM(diag.shape, jnp.float32),
            pltpu.VMEM(linking.shape, jnp.bfloat16),
            pltpu.VMEM(scaling.shape, jnp.float32),
            pltpu.VMEM(residual.shape, jnp.float32),
            pltpu.VMEM(steps.shape, jnp.float32),
            pltpu.SemaphoreType.DMA((5,)),
            pltpu.SemaphoreType.DMA((2,)),
        ],
        compiler_params=pltpu.CompilerParams(vmem_limit_bytes=40 * 2**20),
        name="assemble",
    )(lists, diag, linking, scaling, residual, got, steps)


def on_square(linking, scaling, residual, blocks, step_dx, first_diag):
    n = lax.axis_size("tile")
    diag = first_diag.reshape(-1, BW)
    scaled = (jnp.sqrt(scaling)[:, :, None] * linking).astype(jnp.bfloat16)
    got, steps = exchange(n, scaled, step_dx)
    return assemble(n, blocks.T, diag, linking, scaling, residual, got, steps)


def solution(mesh):
    in_specs = (
        P(("groups", "scen", "tile"), None, None),
        P(("groups", "scen", "tile"), None),
        P(("groups", "scen", "tile"), None),
        P("groups", None),
        P(("groups", "scen"), None),
        P(("groups", "scen")),
    )
    out_specs = (P(("groups", "scen"), "tile"), P(("groups", "scen", "tile"), None))
    tiles_ax, scen_ax = mesh.shape["tile"], mesh.shape["scen"]
    square = scen_ax == tiles_ax and LIST == 2 * tiles_ax
    return jax.shard_map(
        on_square if square else on_device, mesh=mesh, in_specs=in_specs, out_specs=out_specs, check_vma=False
    )
```

```python
import functools

import jax
import jax.numpy as jnp
from jax import lax
from jax.experimental import pallas as pl
from jax.experimental.pallas import tpu as pltpu
from jax.sharding import PartitionSpec as P

BW = 128
LIST = 8
NBLK = 64


def on_device(linking, scaling, residual, blocks, step_dx, first_diag):
    tiles_ax = lax.axis_size("tile")
    scen_ax = lax.axis_size("scen")
    here_scen = lax.axis_index("scen")
    here_tile = lax.axis_index("tile")
    held_scen = linking.shape[0]
    shard_size = tiles_ax * held_scen
    width_rows = step_dx.shape[0]
    width_cols = NBLK // tiles_ax
    per_group = LIST // tiles_ax
    owners_per = scen_ax // tiles_ax
    cap_owner = min(shard_size, (3 * shard_size + 2 * owners_per - 1) // (2 * owners_per))
    slot_count = per_group * per_group * cap_owner
    target_count = width_rows * width_cols
    own_blocks = lax.dynamic_slice_in_dim(
        blocks, (here_scen * tiles_ax + here_tile) * held_scen, held_scen, 0
    )
    low_step = step_dx.astype(jnp.bfloat16)
    full_step = lax.all_gather(low_step, "scen", axis=0, tiled=True)
    picked = full_step[own_blocks].reshape(held_scen, LIST * BW)
    applied = jnp.einsum("src,sc->sr", linking, picked, preferred_element_type=jnp.float32)
    back_step = scaling * (residual - applied)
    scaled = (jnp.sqrt(scaling)[:, :, None] * linking).astype(jnp.bfloat16)
    gram_full = jnp.einsum("sra,src->sac", scaled, scaled, preferred_element_type=jnp.float32)
    gram_tiles = (
        gram_full.reshape(held_scen, LIST, BW, LIST, BW)
        .transpose(0, 1, 3, 2, 4)
        .astype(jnp.bfloat16)
    )
    outgoing = gram_tiles.reshape(held_scen, LIST, per_group, tiles_ax, BW, BW).transpose(
        3, 0, 2, 1, 4, 5
    )
    incoming = lax.all_to_all(outgoing, "tile", split_axis=0, concat_axis=0, tiled=True)
    flat_tiles = incoming.reshape(shard_size * per_group * LIST, BW, BW)
    shard_blocks = blocks.reshape(scen_ax, shard_size, LIST)

    def route_tiles(block_lists):
        col_blocks = jnp.take(block_lists, jnp.arange(per_group) * tiles_ax + here_tile, axis=1)
        row_block = jnp.broadcast_to(
            block_lists[:, None, :], (shard_size, per_group, LIST)
        ).reshape(-1)
        col_block = jnp.broadcast_to(col_blocks[:, :, None], (shard_size, per_group, LIST)).reshape(
            -1
        )
        owner_idx = row_block // width_rows
        hit_table = (owner_idx[:, None] == jnp.arange(scen_ax)[None, :]).astype(jnp.int32)
        before = jnp.cumsum(hit_table, axis=0) - hit_table
        slot_rank = jnp.sum(before * hit_table, axis=1)
        target = row_block % width_rows * width_cols + col_block % width_cols
        return (owner_idx, slot_rank, target)

    own_lists = lax.dynamic_index_in_dim(shard_blocks, here_scen, 0, keepdims=False)
    send_owner, send_rank, unused = route_tiles(own_lists)
    outbox = (
        jnp.zeros((scen_ax, slot_count, BW, BW), jnp.bfloat16)
        .at[send_owner, send_rank]
        .set(flat_tiles)
    )
    received = lax.all_to_all(outbox, "scen", split_axis=0, concat_axis=0, tiled=True)
    all_owner, all_rank, all_target = jax.vmap(route_tiles)(shard_blocks)
    is_mine = all_owner == here_scen
    slot_id = jnp.arange(scen_ax)[:, None] * slot_count + all_rank
    pick_target = (
        (all_target[:, :, None] == jnp.arange(target_count)[None, None, :]) & is_mine[:, :, None]
    ).astype(jnp.float32)
    pick_slot = (slot_id[:, :, None] == jnp.arange(scen_ax * slot_count)[None, None, :]).astype(
        jnp.float32
    )
    select = jnp.einsum("pnt,pnz->tz", pick_target, pick_slot).astype(jnp.bfloat16)
    summed = jnp.dot(
        select, received.reshape(scen_ax * slot_count, BW * BW), preferred_element_type=jnp.float32
    )
    schur_block = (
        summed.reshape(width_rows, width_cols, BW, BW)
        .transpose(0, 2, 1, 3)
        .reshape(width_rows * BW, width_cols * BW)
    )
    rows_global = here_scen * (width_rows * BW) + jnp.arange(width_rows * BW)
    cols_global = here_tile * (width_cols * BW) + jnp.arange(width_cols * BW)
    schur_block = schur_block + jnp.where(
        rows_global[:, None] == cols_global[None, :], first_diag[:, None], 0.0
    )
    return (schur_block, back_step)


MESH = pl.DeviceIdType.MESH
PACK = BW + 16


def pair_masks():
    rows = lax.broadcasted_iota(jnp.int32, (BW, BW), 0)
    cols = lax.broadcasted_iota(jnp.int32, (BW, BW), 1)
    return rows > cols, rows == cols, rows < cols


def exchange_kernel(
    n, held, scaled_ref, step_ref, got_ref, steps_ref, total_ref,
    gathered, parts, end_parts, step_box,
    load_sem, own_sem, pass_sem, chain_sem, end_sem, end_got_sem, part_sem, got_sem, keep_sem,
    step_sem, step_got_sem,
):
    z = lax.axis_index("scen")
    t = lax.axis_index("tile")
    side = z // (n // 2)
    end = side * (n - 1)
    turn = 1 - 2 * side
    inner = (z > 0) & (z < n - 1)
    peers = (lax.rem(t + 2, n), n - 1 - t, t + 1 - 2 * lax.rem(t, 2))
    below, level, above = pair_masks()

    def is_inner(place):
        return (place > 0) & (place < n - 1)

    def hop(source, j, sem, to):
        return pltpu.make_async_remote_copy(
            src_ref=gathered.at[source, j],
            dst_ref=gathered.at[source, j],
            send_sem=sem,
            recv_sem=chain_sem.at[source, j],
            device_id={"scen": to},
            device_id_type=MESH,
        )

    def by_size(packed, act):
        @pl.when(packed)
        def _():
            act(PACK)

        @pl.when(jnp.logical_not(packed))
        def _():
            act(2 * BW)

    def end_send(q, to, size):
        return pltpu.make_async_remote_copy(
            src_ref=end_parts.at[q, to, pl.ds(0, size)],
            dst_ref=parts.at[q, to, pl.ds(0, size)],
            send_sem=end_sem.at[q, to],
            recv_sem=end_got_sem.at[q, to],
            device_id={"scen": end},
            device_id_type=MESH,
        )

    def part_send(q, to, size):
        return pltpu.make_async_remote_copy(
            src_ref=parts.at[q, to, pl.ds(0, size)],
            dst_ref=got_ref.at[t, q, pl.ds(0, size)],
            send_sem=part_sem.at[q, to],
            recv_sem=got_sem.at[t, q],
            device_id={"tile": to},
            device_id_type=MESH,
        )

    def part_arrival(source, q, size):
        return pltpu.make_async_remote_copy(
            src_ref=parts.at[q, source, pl.ds(0, size)],
            dst_ref=got_ref.at[source, q, pl.ds(0, size)],
            send_sem=part_sem.at[q, source],
            recv_sem=got_sem.at[source, q],
            device_id={"tile": source},
            device_id_type=MESH,
        )

    def part_keep(q, size):
        return pltpu.make_async_copy(
            parts.at[q, t, pl.ds(0, size)], got_ref.at[t, q, pl.ds(0, size)], keep_sem.at[q]
        )

    def step_copy(place, to, d):
        return pltpu.make_async_remote_copy(
            src_ref=step_box.at[place],
            dst_ref=step_box.at[place],
            send_sem=step_sem.at[d - 1],
            recv_sem=step_got_sem.at[place],
            device_id={"scen": to},
            device_id_type=MESH,
        )

    def gram(dest, source, j, out, send):
        q = source * held + j
        block = gathered.at[source, j]
        left = jnp.concatenate(
            [block[:, pl.ds(pl.multiple_of((dest + a * n) * BW, BW), BW)] for a in range(2)],
            axis=1,
        )
        turned = left.T
        for to in peers + (t,):
            right = jnp.concatenate(
                [
                    block[:, pl.ds(pl.multiple_of((to + b * n) * BW, BW), BW)]
                    for b in range(2)
                ],
                axis=1,
            )
            tiles = jnp.dot(turned, right, preferred_element_type=jnp.float32)

            @pl.when(dest != to)
            def _():
                out[q, to] = tiles.astype(jnp.bfloat16)

            @pl.when(dest == to)
            def _():
                first, cross, second = tiles[:BW, :BW], tiles[:BW, BW:], tiles[BW:, BW:]
                out[q, to, :BW, :BW] = jnp.where(above, second, first).astype(jnp.bfloat16)
                out[q, to, :BW, BW:] = cross.astype(jnp.bfloat16)
                line = jnp.sum(jnp.where(level, second, 0.0), axis=0, keepdims=True)
                out[q, to, BW:PACK, :BW] = jnp.broadcast_to(line, (PACK - BW, BW)).astype(
                    jnp.bfloat16
                )

            send(q, to)

    def unpack(source, q):
        mixed = got_ref[source, q, :BW, :BW].astype(jnp.float32)
        cross = got_ref[source, q, :BW, BW:].astype(jnp.float32)
        line = got_ref[source, q, BW:PACK, :BW].astype(jnp.float32)[:1]
        flipped = mixed.T
        first = jnp.where(above, flipped, mixed)
        second = jnp.where(above, mixed, jnp.where(below, flipped, line))
        got_ref[source, q, :BW, :BW] = first.astype(jnp.bfloat16)
        got_ref[source, q, BW:, :BW] = cross.T.astype(jnp.bfloat16)
        got_ref[source, q, BW:, BW:] = second.astype(jnp.bfloat16)

    def to_end(source, j):
        def send(q, to):
            by_size(to == end, lambda size: end_send(q, to, size).start())

        gram(end, source, j, end_parts, send)

    def pass_on(q, to):
        if to is t:
            by_size(t == z, lambda size: part_keep(q, size).start())
        else:
            by_size(to == z, lambda size: part_send(q, to, size).start())

    def to_plane(source, j):
        gram(z, source, j, parts, pass_on)

    def finish(p):
        q = lax.rem(z + turn * (p // held) + n, n) * held + p % held
        by_size(t == z, lambda size: part_keep(q, size).wait())
        for to in peers:
            by_size(t == z, lambda size: part_arrival(to, q, size).wait_recv())

        @pl.when(t == z)
        def _():
            for source in range(n):
                unpack(source, q)

    loads = [
        pltpu.make_async_copy(scaled_ref.at[j], gathered.at[z, j], load_sem.at[j])
        for j in range(held)
    ]
    for load in loads:
        load.start()
    barrier = pltpu.get_barrier_semaphore()
    for d in range(1, n):
        pl.semaphore_signal(
            barrier, inc=1, device_id={"scen": lax.rem(z + d, n)}, device_id_type=MESH
        )
        pl.semaphore_signal(
            barrier, inc=1, device_id={"tile": lax.rem(t + d, n)}, device_id_type=MESH
        )
    step_box[z] = step_ref[...].astype(jnp.bfloat16)
    for load in loads:
        load.wait()
    pl.semaphore_wait(barrier, 2 * (n - 1))

    @pl.loop(0, held)
    def _(j):
        for way in (1, -1):

            @pl.when(is_inner(z + way))
            def _():
                hop(z, j, own_sem.at[(1 - way) // 2, j], z + way).start()

        @pl.when(inner)
        def _():
            to_end(z, j)

    for d in range(1, n):
        step_copy(z, lax.rem(z + d, n), d).start()

    @pl.loop(0, held)
    def _(j):
        to_plane(z, j)

    extent = total_ref.shape[1]

    @pl.loop(0, extent // 32)
    def _(i):
        total_ref[pl.ds(pl.multiple_of(i * 32, 32), 32), :] = jnp.zeros((32, extent), jnp.float32)

    @pl.when(inner)
    def _():
        @pl.loop(0, 2 * held * (n - 2))
        def _(i):
            d = 1 + i // (2 * held)
            j = (i // 2) % held
            way = 1 - 2 * (i % 2)
            source = z - way * d
            onward = z + way

            @pl.when((source >= 0) & (source < n))
            def _():
                hop(source, j, pass_sem.at[source, j], z).wait_recv()

                @pl.when(is_inner(onward))
                def _():
                    hop(source, j, pass_sem.at[source, j], onward).start()

                @pl.when(jnp.logical_not(is_inner(onward)))
                def _():
                    to_end(source, j)

                to_plane(source, j)

    @pl.when(jnp.logical_not(inner))
    def _():
        @pl.loop(0, held * (n - 1))
        def _(i):
            q = (z + turn * (1 + i // held)) * held + i % held
            for to in peers + (t,):
                by_size(to == z, lambda size: end_send(q, to, size).wait_recv())
                pass_on(q, to)
            finish(i)

    for d in range(1, n):
        step_copy(z, lax.rem(z + d, n), d).wait_send()
        source = lax.rem(z + d, n)
        step_copy(source, source, d).wait_recv()
    steps_ref[...] = step_box[...].reshape(steps_ref.shape)

    @pl.when(inner)
    def _():
        @pl.loop(0, held * (n - 1))
        def _(p):
            finish(p)

    @pl.loop(held * (n - 1), held * n)
    def _(p):
        finish(p)

    @pl.loop(0, held)
    def _(j):
        for way in (1, -1):

            @pl.when(is_inner(z + way))
            def _():
                hop(z, j, own_sem.at[(1 - way) // 2, j], z + way).wait_send()

    @pl.when(inner)
    def _():
        @pl.loop(0, held)
        def _(j):
            hop(end, j, pass_sem.at[end, j], z + turn).wait_send()

        @pl.loop(0, held * (n - 1))
        def _(i):
            q = (end + turn * (1 + i // held)) * held + i % held
            for to in range(n):
                by_size(to == end, lambda size: end_send(q, to, size).wait_send())

    @pl.loop(0, n * held)
    def _(q):
        for to in peers:
            by_size(to == z, lambda size: part_send(q, to, size).wait_send())


def exchange(n, scaled, step_dx, extent):
    held, rows, width = scaled.shape
    vmem = pl.BlockSpec(memory_space=pltpu.VMEM)
    return pl.pallas_call(
        functools.partial(exchange_kernel, n, held),
        out_shape=(
            jax.ShapeDtypeStruct((n, n * held, 2 * BW, 2 * BW), jnp.bfloat16),
            jax.ShapeDtypeStruct((n * step_dx.shape[0], BW), jnp.bfloat16),
            jax.ShapeDtypeStruct((extent, extent), jnp.float32),
        ),
        in_specs=[pl.BlockSpec(memory_space=pl.ANY), vmem],
        out_specs=(vmem, vmem, vmem),
        scratch_shapes=[
            pltpu.VMEM((n, held, rows, width), jnp.bfloat16),
            pltpu.VMEM((n * held, n, 2 * BW, 2 * BW), jnp.bfloat16),
            pltpu.VMEM((n * held, n, 2 * BW, 2 * BW), jnp.bfloat16),
            pltpu.VMEM((n,) + step_dx.shape, jnp.bfloat16),
            pltpu.SemaphoreType.DMA((held,)),
            pltpu.SemaphoreType.DMA((2, held)),
            pltpu.SemaphoreType.DMA((n, held)),
            pltpu.SemaphoreType.DMA((n, held)),
            pltpu.SemaphoreType.DMA((n * held, n)),
            pltpu.SemaphoreType.DMA((n * held, n)),
            pltpu.SemaphoreType.DMA((n * held, n)),
            pltpu.SemaphoreType.DMA((n, n * held)),
            pltpu.SemaphoreType.DMA((n * held,)),
            pltpu.SemaphoreType.DMA((n - 1,)),
            pltpu.SemaphoreType.DMA((n,)),
        ],
        compiler_params=pltpu.CompilerParams(
            collective_id=0, has_side_effects=True, vmem_limit_bytes=20 * 2**20
        ),
        cost_estimate=pl.CostEstimate(
            flops=60_000_000_000, bytes_accessed=60_000_000_000 // 400, transcendentals=0
        ),
        name="exchange",
    )(scaled, step_dx)


def assemble_kernel(
    n, held, cap, lists_hbm, linking_hbm, scaling_hbm, residual_hbm, diag_hbm, got_ref, steps_ref, given_ref,
    schur_ref, back_ref, total, lists_ref, diag_ref, linking_ref, scaling_ref, residual_ref, wide,
    load_sem, out_sem,
):
    z = lax.axis_index("scen")
    t = lax.axis_index("tile")
    span = cap // 2 * BW

    def store(a, b):
        place = (pl.ds(a * span, span), pl.ds(b * span, span))
        return pltpu.make_async_copy(total.at[place], schur_ref.at[place], out_sem.at[a, b])

    pairs = (
        (lists_hbm, lists_ref), (diag_hbm, diag_ref), (linking_hbm, linking_ref),
        (scaling_hbm, scaling_ref), (residual_hbm, residual_ref),
    )
    loads = [
        pltpu.make_async_copy(far, near, load_sem.at[k]) for k, (far, near) in enumerate(pairs)
    ]
    for load in loads:
        load.start()
    wide[...] = steps_ref[...].astype(jnp.float32)
    loads[0].wait()
    loads[1].wait()
    level = pair_masks()[1]
    for a in range(2):
        for b in range(2):

            @pl.loop(0, n * n * held, unroll=4)
            def _(i):
                source, q = i // (n * held), i % (n * held)
                s = ((q // held) * n + source) * held + q % held
                row = lists_ref[z + a * n, s] - z * cap
                col = lists_ref[t + b * n, s] - t * cap
                place = (
                    pl.ds(pl.multiple_of(row * BW, BW), BW),
                    pl.ds(pl.multiple_of(col * BW, BW), BW),
                )
                tile = got_ref[source, q, a * BW : (a + 1) * BW, b * BW : (b + 1) * BW]
                total[place] += tile.astype(jnp.float32)

            if a == b:

                @pl.when(z == t)
                def _():
                    for r in range(a * cap // 2, (a + 1) * cap // 2):
                        place = (slice(r * BW, (r + 1) * BW), slice(r * BW, (r + 1) * BW))
                        total[place] += jnp.where(level, diag_ref[r : r + 1, :], 0.0)

            store(a, b).start()
    for load in loads[2:]:
        load.wait()
    for j in range(held):
        mine = (z * n + t) * held + j
        picked = jnp.concatenate(
            [wide[pl.ds(lists_ref[k, mine], 1), :] for k in range(2 * n)], axis=1
        )
        applied = lax.dot_general(
            picked.astype(jnp.bfloat16),
            linking_ref[j],
            (((1,), (1,)), ((), ())),
            preferred_element_type=jnp.float32,
        )
        back_ref[j : j + 1, :] = scaling_ref[j : j + 1, :] * (residual_ref[j : j + 1, :] - applied)
    for a in range(2):
        for b in range(2):
            store(a, b).wait()


def assemble(n, lists, linking, scaling, residual, diag, got, steps, given):
    held = linking.shape[0]
    cap = given.shape[0] // BW
    vmem = pl.BlockSpec(memory_space=pltpu.VMEM)
    hbm = pl.BlockSpec(memory_space=pltpu.HBM)
    return pl.pallas_call(
        functools.partial(assemble_kernel, n, held, cap),
        out_shape=(
            jax.ShapeDtypeStruct(given.shape, jnp.float32),
            jax.ShapeDtypeStruct(scaling.shape, jnp.float32),
            jax.ShapeDtypeStruct(given.shape, jnp.float32),
        ),
        in_specs=[hbm] * 5 + [vmem] * 3,
        out_specs=(hbm, vmem, vmem),
        input_output_aliases={7: 2},
        scratch_shapes=[
            pltpu.SMEM(lists.shape, jnp.int32),
            pltpu.VMEM(diag.shape, jnp.float32),
            pltpu.VMEM(linking.shape, jnp.bfloat16),
            pltpu.VMEM(scaling.shape, jnp.float32),
            pltpu.VMEM(residual.shape, jnp.float32),
            pltpu.VMEM(steps.shape, jnp.float32),
            pltpu.SemaphoreType.DMA((5,)),
            pltpu.SemaphoreType.DMA((2, 2)),
        ],
        compiler_params=pltpu.CompilerParams(vmem_limit_bytes=20 * 2**20),
        name="assemble",
    )(lists, linking, scaling, residual, diag, got, steps, given)[:2]


def on_square(linking, scaling, residual, blocks, step_dx, first_diag):
    n = lax.axis_size("tile")
    diag = first_diag.reshape(-1, BW)
    scaled = (jnp.sqrt(scaling)[:, :, None] * linking).astype(jnp.bfloat16)
    got, steps, given = exchange(n, scaled, step_dx, first_diag.shape[0])
    return assemble(n, blocks.T, linking, scaling, residual, diag, got, steps, given)


def solution(mesh):
    in_specs = (
        P(("groups", "scen", "tile"), None, None),
        P(("groups", "scen", "tile"), None),
        P(("groups", "scen", "tile"), None),
        P("groups", None),
        P(("groups", "scen"), None),
        P(("groups", "scen")),
    )
    out_specs = (P(("groups", "scen"), "tile"), P(("groups", "scen", "tile"), None))
    tiles_ax, scen_ax = mesh.shape["tile"], mesh.shape["scen"]
    square = scen_ax == tiles_ax and LIST == 2 * tiles_ax
    return jax.shard_map(
        on_square if square else on_device, mesh=mesh, in_specs=in_specs, out_specs=out_specs, check_vma=False
    )
```

```python
import functools

import jax
import jax.numpy as jnp
from jax import lax
from jax.experimental import pallas as pl
from jax.experimental.pallas import tpu as pltpu
from jax.sharding import PartitionSpec as P

BW = 128
LIST = 8
NBLK = 64


def on_device(linking, scaling, residual, blocks, step_dx, first_diag):
    tiles_ax = lax.axis_size("tile")
    scen_ax = lax.axis_size("scen")
    here_scen = lax.axis_index("scen")
    here_tile = lax.axis_index("tile")
    held_scen = linking.shape[0]
    shard_size = tiles_ax * held_scen
    width_rows = step_dx.shape[0]
    width_cols = NBLK // tiles_ax
    per_group = LIST // tiles_ax
    owners_per = scen_ax // tiles_ax
    cap_owner = min(shard_size, (3 * shard_size + 2 * owners_per - 1) // (2 * owners_per))
    slot_count = per_group * per_group * cap_owner
    target_count = width_rows * width_cols
    own_blocks = lax.dynamic_slice_in_dim(
        blocks, (here_scen * tiles_ax + here_tile) * held_scen, held_scen, 0
    )
    low_step = step_dx.astype(jnp.bfloat16)
    full_step = lax.all_gather(low_step, "scen", axis=0, tiled=True)
    picked = full_step[own_blocks].reshape(held_scen, LIST * BW)
    applied = jnp.einsum("src,sc->sr", linking, picked, preferred_element_type=jnp.float32)
    back_step = scaling * (residual - applied)
    scaled = (jnp.sqrt(scaling)[:, :, None] * linking).astype(jnp.bfloat16)
    gram_full = jnp.einsum("sra,src->sac", scaled, scaled, preferred_element_type=jnp.float32)
    gram_tiles = (
        gram_full.reshape(held_scen, LIST, BW, LIST, BW)
        .transpose(0, 1, 3, 2, 4)
        .astype(jnp.bfloat16)
    )
    outgoing = gram_tiles.reshape(held_scen, LIST, per_group, tiles_ax, BW, BW).transpose(
        3, 0, 2, 1, 4, 5
    )
    incoming = lax.all_to_all(outgoing, "tile", split_axis=0, concat_axis=0, tiled=True)
    flat_tiles = incoming.reshape(shard_size * per_group * LIST, BW, BW)
    shard_blocks = blocks.reshape(scen_ax, shard_size, LIST)

    def route_tiles(block_lists):
        col_blocks = jnp.take(block_lists, jnp.arange(per_group) * tiles_ax + here_tile, axis=1)
        row_block = jnp.broadcast_to(
            block_lists[:, None, :], (shard_size, per_group, LIST)
        ).reshape(-1)
        col_block = jnp.broadcast_to(col_blocks[:, :, None], (shard_size, per_group, LIST)).reshape(
            -1
        )
        owner_idx = row_block // width_rows
        hit_table = (owner_idx[:, None] == jnp.arange(scen_ax)[None, :]).astype(jnp.int32)
        before = jnp.cumsum(hit_table, axis=0) - hit_table
        slot_rank = jnp.sum(before * hit_table, axis=1)
        target = row_block % width_rows * width_cols + col_block % width_cols
        return (owner_idx, slot_rank, target)

    own_lists = lax.dynamic_index_in_dim(shard_blocks, here_scen, 0, keepdims=False)
    send_owner, send_rank, unused = route_tiles(own_lists)
    outbox = (
        jnp.zeros((scen_ax, slot_count, BW, BW), jnp.bfloat16)
        .at[send_owner, send_rank]
        .set(flat_tiles)
    )
    received = lax.all_to_all(outbox, "scen", split_axis=0, concat_axis=0, tiled=True)
    all_owner, all_rank, all_target = jax.vmap(route_tiles)(shard_blocks)
    is_mine = all_owner == here_scen
    slot_id = jnp.arange(scen_ax)[:, None] * slot_count + all_rank
    pick_target = (
        (all_target[:, :, None] == jnp.arange(target_count)[None, None, :]) & is_mine[:, :, None]
    ).astype(jnp.float32)
    pick_slot = (slot_id[:, :, None] == jnp.arange(scen_ax * slot_count)[None, None, :]).astype(
        jnp.float32
    )
    select = jnp.einsum("pnt,pnz->tz", pick_target, pick_slot).astype(jnp.bfloat16)
    summed = jnp.dot(
        select, received.reshape(scen_ax * slot_count, BW * BW), preferred_element_type=jnp.float32
    )
    schur_block = (
        summed.reshape(width_rows, width_cols, BW, BW)
        .transpose(0, 2, 1, 3)
        .reshape(width_rows * BW, width_cols * BW)
    )
    rows_global = here_scen * (width_rows * BW) + jnp.arange(width_rows * BW)
    cols_global = here_tile * (width_cols * BW) + jnp.arange(width_cols * BW)
    schur_block = schur_block + jnp.where(
        rows_global[:, None] == cols_global[None, :], first_diag[:, None], 0.0
    )
    return (schur_block, back_step)


MESH = pl.DeviceIdType.MESH
PACK = BW + 16


def pair_masks():
    rows = lax.broadcasted_iota(jnp.int32, (BW, BW), 0)
    cols = lax.broadcasted_iota(jnp.int32, (BW, BW), 1)
    return rows > cols, rows == cols, rows < cols


def exchange_kernel(
    n, held, scaled_ref, step_ref, got_ref, steps_ref, total_ref,
    gathered, parts, end_parts, step_box,
    load_sem, own_sem, pass_sem, chain_sem, end_sem, end_got_sem, part_sem, got_sem, keep_sem,
    step_sem, step_got_sem,
):
    z = lax.axis_index("scen")
    t = lax.axis_index("tile")
    side = z // (n // 2)
    end = side * (n - 1)
    turn = 1 - 2 * side
    inner = (z > 0) & (z < n - 1)
    peers = (lax.rem(t + 2, n), n - 1 - t, t + 1 - 2 * lax.rem(t, 2))
    below, level, above = pair_masks()

    def is_inner(place):
        return (place > 0) & (place < n - 1)

    def hop(source, j, sem, to):
        return pltpu.make_async_remote_copy(
            src_ref=gathered.at[source, j],
            dst_ref=gathered.at[source, j],
            send_sem=sem,
            recv_sem=chain_sem.at[source, j],
            device_id={"scen": to},
            device_id_type=MESH,
        )

    def by_size(packed, act):
        @pl.when(packed)
        def _():
            act(PACK)

        @pl.when(jnp.logical_not(packed))
        def _():
            act(2 * BW)

    def end_send(q, to, size):
        return pltpu.make_async_remote_copy(
            src_ref=end_parts.at[q, to, pl.ds(0, size)],
            dst_ref=parts.at[q, to, pl.ds(0, size)],
            send_sem=end_sem.at[q, to],
            recv_sem=end_got_sem.at[q, to],
            device_id={"scen": end},
            device_id_type=MESH,
        )

    def part_send(q, to, size):
        return pltpu.make_async_remote_copy(
            src_ref=parts.at[q, to, pl.ds(0, size)],
            dst_ref=got_ref.at[t, q, pl.ds(0, size)],
            send_sem=part_sem.at[q, to],
            recv_sem=got_sem.at[t, q],
            device_id={"tile": to},
            device_id_type=MESH,
        )

    def part_arrival(source, q, size):
        return pltpu.make_async_remote_copy(
            src_ref=parts.at[q, source, pl.ds(0, size)],
            dst_ref=got_ref.at[source, q, pl.ds(0, size)],
            send_sem=part_sem.at[q, source],
            recv_sem=got_sem.at[source, q],
            device_id={"tile": source},
            device_id_type=MESH,
        )

    def part_keep(q, size):
        return pltpu.make_async_copy(
            parts.at[q, t, pl.ds(0, size)], got_ref.at[t, q, pl.ds(0, size)], keep_sem.at[q]
        )

    def step_copy(place, to, d):
        return pltpu.make_async_remote_copy(
            src_ref=step_box.at[place],
            dst_ref=step_box.at[place],
            send_sem=step_sem.at[d - 1],
            recv_sem=step_got_sem.at[place],
            device_id={"scen": to},
            device_id_type=MESH,
        )

    def gram(dest, source, j, out, send):
        q = source * held + j
        block = gathered.at[source, j]
        left = jnp.concatenate(
            [block[:, pl.ds(pl.multiple_of((dest + a * n) * BW, BW), BW)] for a in range(2)],
            axis=1,
        )
        turned = left.T
        for to in peers + (t,):
            right = jnp.concatenate(
                [
                    block[:, pl.ds(pl.multiple_of((to + b * n) * BW, BW), BW)]
                    for b in range(2)
                ],
                axis=1,
            )
            tiles = jnp.dot(turned, right, preferred_element_type=jnp.float32)

            @pl.when(dest != to)
            def _():
                out[q, to] = tiles.astype(jnp.bfloat16)

            @pl.when(dest == to)
            def _():
                first, cross, second = tiles[:BW, :BW], tiles[:BW, BW:], tiles[BW:, BW:]
                out[q, to, :BW, :BW] = jnp.where(above, second, first).astype(jnp.bfloat16)
                out[q, to, :BW, BW:] = cross.astype(jnp.bfloat16)
                line = jnp.sum(jnp.where(level, second, 0.0), axis=0, keepdims=True)
                out[q, to, BW:PACK, :BW] = jnp.broadcast_to(line, (PACK - BW, BW)).astype(
                    jnp.bfloat16
                )

            send(q, to)

    def unpack(source, q):
        mixed = got_ref[source, q, :BW, :BW].astype(jnp.float32)
        cross = got_ref[source, q, :BW, BW:].astype(jnp.float32)
        line = got_ref[source, q, BW:PACK, :BW].astype(jnp.float32)[:1]
        flipped = mixed.T
        first = jnp.where(above, flipped, mixed)
        second = jnp.where(above, mixed, jnp.where(below, flipped, line))
        got_ref[source, q, :BW, :BW] = first.astype(jnp.bfloat16)
        got_ref[source, q, BW:, :BW] = cross.T.astype(jnp.bfloat16)
        got_ref[source, q, BW:, BW:] = second.astype(jnp.bfloat16)

    def to_end(source, j):
        def send(q, to):
            by_size(to == end, lambda size: end_send(q, to, size).start())

        gram(end, source, j, end_parts, send)

    def pass_on(q, to):
        if to is t:
            by_size(t == z, lambda size: part_keep(q, size).start())
        else:
            by_size(to == z, lambda size: part_send(q, to, size).start())

    def to_plane(source, j):
        gram(z, source, j, parts, pass_on)

    def finish(p):
        q = lax.rem(z + turn * (p // held) + n, n) * held + p % held
        by_size(t == z, lambda size: part_keep(q, size).wait())
        for to in peers:
            by_size(t == z, lambda size: part_arrival(to, q, size).wait_recv())

        @pl.when(t == z)
        def _():
            for source in range(n):
                unpack(source, q)

    loads = [
        pltpu.make_async_copy(scaled_ref.at[j], gathered.at[z, j], load_sem.at[j])
        for j in range(held)
    ]
    for load in loads:
        load.start()
    barrier = pltpu.get_barrier_semaphore()
    for d in range(1, n):
        pl.semaphore_signal(
            barrier, inc=1, device_id={"scen": lax.rem(z + d, n)}, device_id_type=MESH
        )
        pl.semaphore_signal(
            barrier, inc=1, device_id={"tile": lax.rem(t + d, n)}, device_id_type=MESH
        )
    step_box[z] = step_ref[...].astype(jnp.bfloat16)
    for load in loads:
        load.wait()
    pl.semaphore_wait(barrier, 2 * (n - 1))

    @pl.loop(0, held)
    def _(j):
        for way in (1, -1):

            @pl.when(is_inner(z + way))
            def _():
                hop(z, j, own_sem.at[(1 - way) // 2, j], z + way).start()

        @pl.when(inner)
        def _():
            to_end(z, j)

    for d in range(1, n):
        step_copy(z, lax.rem(z + d, n), d).start()

    @pl.loop(0, held)
    def _(j):
        to_plane(z, j)

    extent = total_ref.shape[1]

    @pl.loop(0, extent // 32)
    def _(i):
        total_ref[pl.ds(pl.multiple_of(i * 32, 32), 32), :] = jnp.zeros((32, extent), jnp.float32)

    @pl.when(inner)
    def _():
        @pl.loop(0, 2 * held * (n - 2))
        def _(i):
            d = 1 + i // (2 * held)
            j = (i // 2) % held
            way = 1 - 2 * (i % 2)
            source = z - way * d
            onward = z + way

            @pl.when((source >= 0) & (source < n))
            def _():
                hop(source, j, pass_sem.at[source, j], z).wait_recv()

                @pl.when(is_inner(onward))
                def _():
                    hop(source, j, pass_sem.at[source, j], onward).start()

                @pl.when(jnp.logical_not(is_inner(onward)))
                def _():
                    to_end(source, j)

                to_plane(source, j)

    @pl.when(jnp.logical_not(inner))
    def _():
        @pl.loop(0, held * (n - 1))
        def _(i):
            q = (z + turn * (1 + i // held)) * held + i % held
            for to in peers + (t,):
                by_size(to == z, lambda size: end_send(q, to, size).wait_recv())
                pass_on(q, to)
            finish(i)

    for d in range(1, n):
        step_copy(z, lax.rem(z + d, n), d).wait_send()
        source = lax.rem(z + d, n)
        step_copy(source, source, d).wait_recv()
    steps_ref[...] = step_box[...].reshape(steps_ref.shape)

    @pl.when(inner)
    def _():
        @pl.loop(0, held * (n - 1))
        def _(p):
            finish(p)

    @pl.loop(held * (n - 1), held * n)
    def _(p):
        finish(p)

    @pl.loop(0, held)
    def _(j):
        for way in (1, -1):

            @pl.when(is_inner(z + way))
            def _():
                hop(z, j, own_sem.at[(1 - way) // 2, j], z + way).wait_send()

    @pl.when(inner)
    def _():
        @pl.loop(0, held)
        def _(j):
            hop(end, j, pass_sem.at[end, j], z + turn).wait_send()

        @pl.loop(0, held * (n - 1))
        def _(i):
            q = (end + turn * (1 + i // held)) * held + i % held
            for to in range(n):
                by_size(to == end, lambda size: end_send(q, to, size).wait_send())

    @pl.loop(0, n * held)
    def _(q):
        for to in peers:
            by_size(to == z, lambda size: part_send(q, to, size).wait_send())


def exchange(n, scaled, step_dx, extent):
    held, rows, width = scaled.shape
    vmem = pl.BlockSpec(memory_space=pltpu.VMEM)
    return pl.pallas_call(
        functools.partial(exchange_kernel, n, held),
        out_shape=(
            jax.ShapeDtypeStruct((n, n * held, 2 * BW, 2 * BW), jnp.bfloat16),
            jax.ShapeDtypeStruct((n * step_dx.shape[0], BW), jnp.bfloat16),
            jax.ShapeDtypeStruct((extent, extent), jnp.float32),
        ),
        in_specs=[pl.BlockSpec(memory_space=pl.ANY), vmem],
        out_specs=(vmem, vmem, vmem),
        scratch_shapes=[
            pltpu.VMEM((n, held, rows, width), jnp.bfloat16),
            pltpu.VMEM((n * held, n, 2 * BW, 2 * BW), jnp.bfloat16),
            pltpu.VMEM((n * held, n, 2 * BW, 2 * BW), jnp.bfloat16),
            pltpu.VMEM((n,) + step_dx.shape, jnp.bfloat16),
            pltpu.SemaphoreType.DMA((held,)),
            pltpu.SemaphoreType.DMA((2, held)),
            pltpu.SemaphoreType.DMA((n, held)),
            pltpu.SemaphoreType.DMA((n, held)),
            pltpu.SemaphoreType.DMA((n * held, n)),
            pltpu.SemaphoreType.DMA((n * held, n)),
            pltpu.SemaphoreType.DMA((n * held, n)),
            pltpu.SemaphoreType.DMA((n, n * held)),
            pltpu.SemaphoreType.DMA((n * held,)),
            pltpu.SemaphoreType.DMA((n - 1,)),
            pltpu.SemaphoreType.DMA((n,)),
        ],
        compiler_params=pltpu.CompilerParams(
            collective_id=0, has_side_effects=True, vmem_limit_bytes=20 * 2**20
        ),
        cost_estimate=pl.CostEstimate(
            flops=60_000_000_000, bytes_accessed=60_000_000_000 // 400, transcendentals=0
        ),
        name="exchange",
    )(scaled, step_dx)


def assemble_kernel(
    n, held, cap, lists_hbm, linking_hbm, scaling_hbm, residual_hbm, diag_hbm, got_ref, steps_ref, given_ref,
    schur_ref, back_ref, total, lists_ref, diag_ref, linking_ref, scaling_ref, residual_ref, wide,
    load_sem, out_sem,
):
    z = lax.axis_index("scen")
    t = lax.axis_index("tile")
    span = cap // 2 * BW

    def store(a, b):
        place = (pl.ds(a * span, span), pl.ds(b * span, span))
        return pltpu.make_async_copy(total.at[place], schur_ref.at[place], out_sem.at[a, b])

    pairs = (
        (lists_hbm, lists_ref), (diag_hbm, diag_ref), (linking_hbm, linking_ref),
        (scaling_hbm, scaling_ref), (residual_hbm, residual_ref),
    )
    loads = [
        pltpu.make_async_copy(far, near, load_sem.at[k]) for k, (far, near) in enumerate(pairs)
    ]
    for load in loads:
        load.start()
    wide[...] = steps_ref[...].astype(jnp.float32)
    loads[0].wait()
    loads[1].wait()
    level = pair_masks()[1]
    for a in range(2):
        for b in range(2):

            @pl.loop(0, n * n * held, unroll=8)
            def _(i):
                source, q = i // (n * held), i % (n * held)
                s = ((q // held) * n + source) * held + q % held
                row = lists_ref[z + a * n, s] - z * cap
                col = lists_ref[t + b * n, s] - t * cap
                place = (
                    pl.ds(pl.multiple_of(row * BW, BW), BW),
                    pl.ds(pl.multiple_of(col * BW, BW), BW),
                )
                tile = got_ref[source, q, a * BW : (a + 1) * BW, b * BW : (b + 1) * BW]
                total[place] += tile.astype(jnp.float32)

            if a == b:

                @pl.when(z == t)
                def _():
                    for r in range(a * cap // 2, (a + 1) * cap // 2):
                        place = (slice(r * BW, (r + 1) * BW), slice(r * BW, (r + 1) * BW))
                        total[place] += jnp.where(level, diag_ref[r : r + 1, :], 0.0)

            store(a, b).start()
    for load in loads[2:]:
        load.wait()
    for j in range(held):
        mine = (z * n + t) * held + j
        picked = jnp.concatenate(
            [wide[pl.ds(lists_ref[k, mine], 1), :] for k in range(2 * n)], axis=1
        )
        applied = lax.dot_general(
            picked.astype(jnp.bfloat16),
            linking_ref[j],
            (((1,), (1,)), ((), ())),
            preferred_element_type=jnp.float32,
        )
        back_ref[j : j + 1, :] = scaling_ref[j : j + 1, :] * (residual_ref[j : j + 1, :] - applied)
    for a in range(2):
        for b in range(2):
            store(a, b).wait()


def assemble(n, lists, linking, scaling, residual, diag, got, steps, given):
    held = linking.shape[0]
    cap = given.shape[0] // BW
    vmem = pl.BlockSpec(memory_space=pltpu.VMEM)
    hbm = pl.BlockSpec(memory_space=pltpu.HBM)
    return pl.pallas_call(
        functools.partial(assemble_kernel, n, held, cap),
        out_shape=(
            jax.ShapeDtypeStruct(given.shape, jnp.float32),
            jax.ShapeDtypeStruct(scaling.shape, jnp.float32),
            jax.ShapeDtypeStruct(given.shape, jnp.float32),
        ),
        in_specs=[hbm] * 5 + [vmem] * 3,
        out_specs=(hbm, vmem, vmem),
        input_output_aliases={7: 2},
        scratch_shapes=[
            pltpu.SMEM(lists.shape, jnp.int32),
            pltpu.VMEM(diag.shape, jnp.float32),
            pltpu.VMEM(linking.shape, jnp.bfloat16),
            pltpu.VMEM(scaling.shape, jnp.float32),
            pltpu.VMEM(residual.shape, jnp.float32),
            pltpu.VMEM(steps.shape, jnp.float32),
            pltpu.SemaphoreType.DMA((5,)),
            pltpu.SemaphoreType.DMA((2, 2)),
        ],
        compiler_params=pltpu.CompilerParams(vmem_limit_bytes=20 * 2**20),
        name="assemble",
    )(lists, linking, scaling, residual, diag, got, steps, given)[:2]


def on_square(linking, scaling, residual, blocks, step_dx, first_diag):
    n = lax.axis_size("tile")
    diag = first_diag.reshape(-1, BW)
    scaled = (jnp.sqrt(scaling)[:, :, None] * linking).astype(jnp.bfloat16)
    got, steps, given = exchange(n, scaled, step_dx, first_diag.shape[0])
    return assemble(n, blocks.T, linking, scaling, residual, diag, got, steps, given)


def solution(mesh):
    in_specs = (
        P(("groups", "scen", "tile"), None, None),
        P(("groups", "scen", "tile"), None),
        P(("groups", "scen", "tile"), None),
        P("groups", None),
        P(("groups", "scen"), None),
        P(("groups", "scen")),
    )
    out_specs = (P(("groups", "scen"), "tile"), P(("groups", "scen", "tile"), None))
    tiles_ax, scen_ax = mesh.shape["tile"], mesh.shape["scen"]
    square = scen_ax == tiles_ax and LIST == 2 * tiles_ax
    return jax.shard_map(
        on_square if square else on_device, mesh=mesh, in_specs=in_specs, out_specs=out_specs, check_vma=False
    )
```
